256 devices in a mesh: rep: 16 (over z_hi, y, core), shard: 16 (over z_lo, x).
Axes of the slice: x: 4, y: 4, z: 8 (z_hi: 2, z_lo: 4; z = z_hi * 4 + z_lo), core: 2. Of those that a mesh axis runs over, the one named last changes fastest.
Arguments:
- cell_features: bfloat16 [16, 8192, 1024], P('rep', 'shard'), may hold values from -10 to 10
- upstream: bfloat16 [16, 8192, 1024], P('rep', 'shard'), may hold values from -0.119628906 to 0.119628906
- qkv_weight: bfloat16 [16, 1024, 3072], P('rep', 'shard'), may hold values from -0.1875 to 0.1875
- out_weight: bfloat16 [16, 1024, 1024], P('rep', 'shard'), may hold values from -0.1875 to 0.1875
- momentum: float32 [16, 1024, 1024], P('rep', 'shard'), may hold values from -4 to 4
- key_tiles: int32 [16, 64, 6], P('rep'), may hold values from 0 to 63, as said below
- live_blocks: int32 [16, 64], P('rep'), may hold values from 1 to 6
- step_index: int32 [], replicated, may hold values from 0 to 999
Outputs:
- layer_out: bfloat16 [16, 8192, 1024], P('rep', 'shard')
- new_weight: bfloat16 [16, 1024, 1024], P('rep', 'shard')
- new_momentum: float32 [16, 1024, 1024], P('rep', 'shard')
The draws below stay inside these ranges and needn't reach their ends.
Inputs may be any that keep to these rules, and one draw needn't show every extreme that they name: `key_tiles`: every entry names a tile of its group. Of the 24 entries of device d's 4 query tiles (tiles d*4 to (d+1)*4 - 1), exactly 12 name tiles of device d itself (tile // 4 == d); of the others at most 1 name tiles of any one other device, and in every draw some device is named exactly 1 times.
All inputs are finite; a program needn't handle non-finite values.
Results may differ from the reference program's by a relative error of at most 0.025.
Values may be sent and summed in bfloat16 or wider, within the bound.
A program may use at most 128 MiB of HBM per device.

```python
import jax
import jax.numpy as jnp
from jax import lax

D = 1024
HEADS = 16
HEAD_DIM = 64
TILE = 128
KB = 6
TILES_DEV = 4
GTILES = 64
CELLS = 8192
REPLICAS = 16
LOCAL = 12
REMOTE = 12
CAP = 1
N_REP = 16
N_SHARD = 16


def draw_cell_features(key, part):
    first_key = jax.random.fold_in(key, 0)
    base = jax.random.normal(first_key, (REPLICAS, CELLS, D), jnp.float32)
    return jnp.clip(base, -10.0, 10.0).astype(jnp.bfloat16)


def draw_key_tiles(key, part):
    device_keys = jax.random.split(jax.random.fold_in(key, 7), N_REP * N_SHARD)
    device_numbers = jnp.arange(N_REP * N_SHARD, dtype=jnp.int32) % N_SHARD

    def one_device(device_key, device):
        perm_key, shuffle_key, tile_key, local_key = jax.random.split(device_key, 4)
        others = jnp.arange(1, N_SHARD, dtype=jnp.int32)
        perms = jax.vmap(lambda inner: jax.random.permutation(inner, others))(jax.random.split(perm_key, CAP))
        offsets = perms.reshape(-1)[:REMOTE]
        owners = (device + offsets) % N_SHARD
        remote_tiles = owners * TILES_DEV + jax.random.randint(tile_key, (REMOTE,), 0, TILES_DEV)
        local_tiles = device * TILES_DEV + jax.random.randint(local_key, (LOCAL,), 0, TILES_DEV)
        entries = jnp.concatenate([local_tiles, remote_tiles]).astype(jnp.int32)
        return jax.random.permutation(shuffle_key, entries).astype(jnp.int32)
    return jax.vmap(one_device)(device_keys, device_numbers).reshape(N_REP, N_SHARD * TILES_DEV, KB)


def plant(array, rng, smallest, largest):
    longest = array.shape.index(max(array.shape))
    spots = []
    for shift in (0, 1):
        where = [jax.random.randint(jax.random.fold_in(rng, axis), (), 0, length) for axis, length in enumerate(array.shape)]
        where[longest] = (where[longest] + shift) % array.shape[longest]
        spots.append(tuple(where))
    return array.at[spots[0]].set(smallest).at[spots[1]].set(largest)


def level_of(key, shape, cuts, low, largest):
    level, own = 1.0, jax.random.fold_in(key, 6)
    for axis_at, parts in cuts:
        steps = jnp.exp(jax.random.uniform(jax.random.fold_in(own, axis_at), (parts,), jnp.float32, low / len(cuts), largest / len(cuts)))
        level = level * jnp.repeat(steps, shape[axis_at] // parts).reshape([-1 if axis == axis_at else 1 for axis in range(len(shape))])
    return level


def centred(key, shape, scale, bound, shards=(), held_as=jnp.bfloat16):
    result = jax.random.normal(key, shape, jnp.float32) * scale
    if len(shards) > 0:
        result = level_of(key, shape, shards, -0.22, 0.18) * result
    return jnp.clip(result, min=-bound, max=bound).astype(held_as)


def setup_inputs(seed: int = 0) -> dict:
    splits = jax.random.split(jax.random.key(seed), 9)
    return {
        "cell_features": draw_cell_features(jax.random.fold_in(splits[8], 71), 0),
        "upstream": centred(splits[1], (REPLICAS, CELLS, D), 0.02, 0.119628906, ((0, 16), (1, 16))),
        "qkv_weight": centred(splits[2], (REPLICAS, D, 3 * D), D ** -0.5, 0.1875, ((0, 16), (1, 16))),
        "out_weight": centred(splits[3], (REPLICAS, D, D), D ** -0.5, 0.1875, ((0, 16), (1, 16))),
        "momentum": centred(splits[4], (REPLICAS, D, D), 0.5, 4.0, ((0, 16), (1, 16)), jnp.float32),
        "key_tiles": draw_key_tiles(jax.random.fold_in(splits[8], 71), 0),
        "live_blocks": plant(jax.random.randint(splits[6], (REPLICAS, GTILES), 1, KB + 1), jax.random.fold_in(splits[6], 1), 1, KB).astype(jnp.int32),
        "step_index": jax.random.randint(splits[7], (), 0, 1000).astype(jnp.int32),
    }


momentum_beta = 0.9


def attend_tile(query_tile, key_value, live_count):
    model_width = query_tile.shape[1]
    query_split = query_tile.reshape(TILE, HEADS, HEAD_DIM).astype(jnp.float32)
    keys_split = key_value[:, :model_width].reshape(KB * TILE, HEADS, HEAD_DIM).astype(jnp.float32)
    values_split = key_value[:, model_width:].reshape(KB * TILE, HEADS, HEAD_DIM).astype(jnp.float32)
    scores = jnp.einsum("qhd,khd->hqk", query_split, keys_split) * (HEAD_DIM ** -0.5)
    usable = (jnp.arange(KB * TILE, dtype=jnp.int32) // TILE) < live_count
    scores = jnp.where(usable[None, None, :], scores, jnp.float32(-1e30))
    row_max = jnp.max(scores, axis=2, keepdims=True)
    exponent = jnp.exp(scores - row_max)
    probabilities = (exponent / jnp.sum(exponent, axis=2, keepdims=True)).astype(jnp.bfloat16)
    mixture = jnp.einsum("hqk,khd->qhd", probabilities.astype(jnp.float32), values_split)
    return mixture.reshape(TILE, model_width).astype(jnp.bfloat16)


def replica_step(inputs, learn_rate):
    features, cotangent, qkv, weight, moment, tile_lists, live = inputs
    projected = jnp.dot(features, qkv, preferred_element_type=jnp.float32).astype(jnp.bfloat16)
    query = projected[:, :D].reshape(GTILES, TILE, D)
    key_value = projected[:, D:].reshape(GTILES, TILE, 2 * D)

    def one_tile(element):
        query_tile, listed, live_count = element
        gathered = key_value[listed].reshape(KB * TILE, 2 * D)
        return attend_tile(query_tile, gathered, live_count)

    attended = lax.map(one_tile, (query, tile_lists, live)).reshape(CELLS, D)
    product = jnp.dot(attended, weight, preferred_element_type=jnp.float32)
    layer_out = (features.astype(jnp.float32) + product).astype(jnp.bfloat16)
    gradient = jnp.dot(attended.T, cotangent, preferred_element_type=jnp.float32)
    velocity = momentum_beta * moment + gradient
    stepped = (weight.astype(jnp.float32) - learn_rate * velocity).astype(jnp.bfloat16)
    return layer_out, stepped, velocity


def reference(cell_features, upstream, qkv_weight, out_weight, momentum, key_tiles, live_blocks, step_index):
    learn_rate = jnp.float32(50.0) / (jnp.float32(500.0) + step_index.astype(jnp.float32))
    layer_out, stepped, velocity = lax.map(lambda inputs: replica_step(inputs, learn_rate), (cell_features, upstream, qkv_weight, out_weight, momentum, key_tiles, live_blocks))
    bit_count = N_REP.bit_length() - 1
    bit_number = (step_index % bit_count).astype(jnp.int32)
    partner = jnp.bitwise_xor(jnp.arange(N_REP, dtype=jnp.int32), jnp.left_shift(jnp.int32(1), bit_number).astype(jnp.int32))
    new_weight = (0.5 * (stepped.astype(jnp.float32) + stepped[partner].astype(jnp.float32))).astype(jnp.bfloat16)
    new_momentum = 0.5 * (velocity + velocity[partner])
    return layer_out, new_weight, new_momentum
```

```python
import jax
import jax.numpy as jnp
from jax import lax
from jax.experimental import pallas as pl
from jax.experimental.pallas import tpu as pltpu
from jax.sharding import PartitionSpec as P

HEADS = 16
HEAD_DIM = 64
TILE = 128
KB = 6
TILES = 4
NX = 4
NZ = 4
SHARDS = NX * NZ
GROUPS = 4
D = 1024
GW = D // GROUPS
BLOCK = D // SHARDS
ROWS = TILES * TILE
TABLE = TILES + SHARDS - 1
MESH = pl.DeviceIdType.MESH

momentum_beta = 0.9


def at(z, x):
    return {"shard": z * NX + x}


def layer_kernel(
    pick_ref, slots_ref, live_ref, rate_ref, x_ref, up_ref, w_ref, ow_ref, mom_ref,
    layer_ref, pair_ref, vel_ref,
    table, packed, wbuf, owbuf, kbuf, vbuf, qbuf, att, grad, first, partial, second, total,
    fs, fr, zs, zr, xs, xr, os_, or_, gs, gr, hs, hr,
):
    me = lax.axis_index("shard")
    z, x = lax.div(me, NX), lax.rem(me, NX)

    barrier = pltpu.get_barrier_semaphore()
    for k in range(1, SHARDS):
        pl.semaphore_signal(
            barrier, 1, device_id={"shard": lax.rem(me + k, SHARDS)}, device_id_type=MESH
        )

    for t in range(TILES):
        table[t] = x_ref[t]
    for g in range(GROUPS):
        for part in range(3):
            wbuf[g, z, x, :, pl.ds(part * GW, GW)] = w_ref[:, pl.ds(part * D + g * GW, GW)]
    owbuf[z, x] = ow_ref[...]
    pl.semaphore_wait(barrier, SHARDS - 1)

    def along_z(step, up, sending):
        from_z = z if sending else (z - 1 if up else z + 1)
        block = from_z - step if up else from_z + step
        valid = (block >= 0) & (block < NZ)
        if sending:
            valid &= (z < NZ - 1) if up else (z > 0)
        block = lax.rem(block + 2 * NZ, NZ)
        to = lax.rem(z + (1 if up else NZ - 1), NZ)
        i = step * 2 + (0 if up else 1)
        pair = [
            pltpu.make_async_remote_copy(
                src_ref=b, dst_ref=b, send_sem=s.at[j], recv_sem=r.at[j],
                device_id=at(to, x), device_id_type=MESH,
            )
            for b, s, r, j in (
                (wbuf.at[:, block, x], zs, zr, i),
                (owbuf.at[block, x], os_, or_, i),
            )
        ]
        return valid, pair

    def start_z(step):
        for up in (True, False):
            valid, pair = along_z(step, up, True)

            @pl.when(valid)
            def _():
                for c in pair:
                    c.start()

    def wait_z(step):
        for up in (True, False):
            valid, pair = along_z(step, up, False)

            @pl.when(valid)
            def _():
                for c in pair:
                    c.wait_recv()

    def end_z(step):
        for up in (True, False):
            valid, pair = along_z(step, up, True)

            @pl.when(valid)
            def _():
                for c in pair:
                    c.wait_send()

    right, left = lax.rem(x + 1, NX), lax.rem(x + NX - 1, NX)

    def ring(buf, forward, sems, base):
        ssem, rsem = sems
        out = []
        for way, to, back in ((0, right, left), (1, left, right)):
            if forward:
                half = pl.ds(way * (NZ // 2), NZ // 2)
                far = lax.rem(x + NX // 2, NX)
                src, dst = buf.at[half, back], buf.at[half, far]
            else:
                src, dst = buf.at[:, x], buf.at[:, back]
            i = base + (2 if forward else 0) + way
            pair = [
                pltpu.make_async_remote_copy(
                    src_ref=ref, dst_ref=ref, send_sem=ssem.at[i], recv_sem=rsem.at[i],
                    device_id=at(z, to), device_id_type=MESH,
                )
                for ref in (src, dst)
            ]
            out.append(pair)
        return out

    def group_ring(g, forward):
        return ring(wbuf.at[g], forward, (xs, xr), g * 4)

    def out_ring(forward):
        return ring(owbuf, forward, (os_, or_), 6)

    start_z(0)

    def tile_copy(k):
        return pltpu.make_async_remote_copy(
            src_ref=packed.at[k - 1], dst_ref=table.at[TILES + k - 1],
            send_sem=fs.at[k - 1], recv_sem=fr.at[k - 1],
            device_id={"shard": lax.rem(me + k, SHARDS)}, device_id_type=MESH,
        )

    def send_tile(k, c):
        t = pick_ref[lax.rem(me + k, SHARDS)]
        packed[k - 1] = x_ref[t]
        tile_copy(k).start()
        return c

    lax.fori_loop(1, SHARDS, send_tile, 0)

    wait_z(0)
    start_z(1)
    wait_z(1)
    start_z(2)
    wait_z(2)
    for g in range(GROUPS):
        for mine, _ in group_ring(g, False):
            mine.start()
    for g in range(GROUPS):
        for _, lands in group_ring(g, False):
            lands.wait_recv()
        for mine, _ in group_ring(g, True):
            mine.start()
    for mine, _ in out_ring(False):
        mine.start()

    def wait_tile(k, c):
        tile_copy(k).wait_recv()
        return c

    lax.fori_loop(1, SHARDS, wait_tile, 0)
    for _, lands in out_ring(False):
        lands.wait_recv()
    for mine, _ in out_ring(True):
        mine.start()

    lane_head = lax.broadcasted_iota(jnp.int32, (TILE, GW), 1) // HEAD_DIM
    slot_of = lax.broadcasted_iota(jnp.int32, (1, KB * TILE), 1) // TILE
    nt = (((1,), (1,)), ((), ()))
    tn = (((0,), (0,)), ((), ()))

    def first_copy(g, step):
        to = lax.rem(x + step, NX)
        i = g * (NX - 1) + step - 1
        return pltpu.make_async_remote_copy(
            src_ref=grad.at[g, to], dst_ref=first.at[g, step - 1],
            send_sem=gs.at[i], recv_sem=gr.at[i],
            device_id=at(z, to), device_id_type=MESH,
        )

    def second_copy(g, slot):
        return pltpu.make_async_remote_copy(
            src_ref=partial.at[g], dst_ref=second.at[slot],
            send_sem=hs.at[g], recv_sem=hr.at[slot],
            device_id=at(g, x), device_id_type=MESH,
        )

    def finish_first(g):
        summed = grad[g, x].astype(jnp.float32)
        for step in range(1, NX):
            first_copy(g, step).wait_recv()
            summed += first[g, step - 1].astype(jnp.float32)

        @pl.when(z == g)
        def _():
            total[...] = summed

        @pl.when(z != g)
        def _():
            partial[g] = summed.astype(jnp.bfloat16)
            second_copy(g, lax.rem(z - g + NZ, NZ) - 1).start()

    def group(g, c):
        for way in range(2):
            for _, lands in (group_ring(g, True)[way],):
                lands.wait_recv()
        queries = jnp.dot(
            table[0:TILES].reshape(ROWS, D), wbuf[g, :, :, :, 0:GW].reshape(D, GW),
            preferred_element_type=jnp.float32,
        ).astype(jnp.bfloat16)
        qbuf[...] = queries * jnp.bfloat16(HEAD_DIM ** -0.5)

        def project(t, c):
            both = jnp.dot(
                table[t], wbuf[g, :, :, :, GW : 3 * GW].reshape(D, 2 * GW),
                preferred_element_type=jnp.float32,
            ).astype(jnp.bfloat16)
            kbuf[t] = both[:, 0:GW]
            vbuf[t] = both[:, GW : 2 * GW]
            return c

        lax.fori_loop(0, TABLE, project, 0)

        def attend(i, c):
            live = live_ref[me * TILES + i]
            keys, values = [], []
            for j in range(KB):
                slot = slots_ref[me, i * KB + j]
                keys.append(kbuf[slot])
                values.append(vbuf[slot])
            q = qbuf[pl.ds(pl.multiple_of(i * TILE, TILE), TILE), :]
            masked = jnp.concatenate(
                [jnp.where(lane_head == h, q, jnp.bfloat16(0)) for h in range(GW // HEAD_DIM)], axis=0
            )
            scores = lax.dot_general(
                masked, jnp.concatenate(keys, axis=0), nt, preferred_element_type=jnp.float32
            )
            scores = jnp.where(slot_of < live, scores, jnp.float32(-1e30))
            exponent = jnp.exp(scores - jnp.max(scores, axis=1, keepdims=True))
            scale = 1.0 / jnp.sum(exponent, axis=1, keepdims=True)
            mixed = jnp.dot(
                exponent.astype(jnp.bfloat16), jnp.concatenate(values, axis=0),
                preferred_element_type=jnp.float32,
            ) * scale
            joined = jnp.zeros((TILE, GW), jnp.float32)
            for h in range(GW // HEAD_DIM):
                joined = jnp.where(lane_head == h, mixed[h * TILE : (h + 1) * TILE], joined)
            att[g, pl.ds(pl.multiple_of(i * TILE, TILE), TILE), :] = joined.astype(jnp.bfloat16)
            return c

        lax.fori_loop(0, TILES, attend, 0)
        grad[g] = (
            lax.dot_general(att[g], up_ref[...], tn, preferred_element_type=jnp.float32)
            .astype(jnp.bfloat16)
            .reshape(NX, BLOCK, D)
        )
        for step in range(1, NX):
            first_copy(g, step).start()

        @pl.when(g > 0)
        def _():
            finish_first(g - 1)

        return c

    lax.fori_loop(0, GROUPS, group, 0)

    for _, lands in out_ring(True):
        lands.wait_recv()

    def project_out(i, c):
        rows = pl.ds(pl.multiple_of(i * TILE, TILE), TILE)
        product = table[i].astype(jnp.float32)
        for g in range(GROUPS):
            product += jnp.dot(
                att[g, rows, :], owbuf[g].reshape(GW, D), preferred_element_type=jnp.float32
            )
        layer_ref[rows, :] = product.astype(jnp.bfloat16)
        return c

    finish_first(GROUPS - 1)
    lax.fori_loop(0, TILES, project_out, 0)

    summed = total[...]
    for slot in range(NZ - 1):
        second_copy(0, slot).wait_recv()
        summed += second[slot].astype(jnp.float32)
    velocity = momentum_beta * mom_ref[...] + summed
    stepped = ow_ref[...].astype(jnp.float32) - rate_ref[0] * velocity
    vel_ref[...] = velocity
    pair_ref[0] = stepped.astype(jnp.bfloat16)
    pair_ref[1] = velocity.astype(jnp.bfloat16)

    for step in range(NZ - 1):
        end_z(step)
    for forward in (False, True):
        for g in range(GROUPS):
            for mine, _ in group_ring(g, forward):
                mine.wait_send()
        for mine, _ in out_ring(forward):
            mine.wait_send()

    def sent_tile(k, c):
        tile_copy(k).wait_send()
        return c

    lax.fori_loop(1, SHARDS, sent_tile, 0)
    for g in range(GROUPS):
        for step in range(1, NX):
            first_copy(g, step).wait_send()

        @pl.when(z != g)
        def _():
            second_copy(g, 0).wait_send()


def run_layer(pick, slots, live, rate, features, upstream, qkv, out, momentum):
    vmem = pl.BlockSpec(memory_space=pltpu.VMEM)
    smem = pl.BlockSpec(memory_space=pltpu.SMEM)
    dma = pltpu.SemaphoreType.DMA
    bf16, f32 = jnp.bfloat16, jnp.float32
    return pl.pallas_call(
        layer_kernel,
        name="layer",
        out_shape=(
            jax.ShapeDtypeStruct((ROWS, D), bf16),
            jax.ShapeDtypeStruct((2, BLOCK, D), bf16),
            jax.ShapeDtypeStruct((BLOCK, D), f32),
        ),
        in_specs=[smem] * 4 + [vmem] * 5,
        out_specs=(vmem, vmem, vmem),
        scratch_shapes=[
            pltpu.VMEM((TABLE, TILE, D), bf16),
            pltpu.VMEM((SHARDS - 1, TILE, D), bf16),
            pltpu.VMEM((GROUPS, NZ, NX, BLOCK, 3 * GW), bf16),
            pltpu.VMEM((NZ, NX, BLOCK, D), bf16),
            pltpu.VMEM((TABLE, TILE, GW), bf16),
            pltpu.VMEM((TABLE, TILE, GW), bf16),
            pltpu.VMEM((ROWS, GW), bf16),
            pltpu.VMEM((GROUPS, ROWS, GW), bf16),
            pltpu.VMEM((GROUPS, NX, BLOCK, D), bf16),
            pltpu.VMEM((GROUPS, NX - 1, BLOCK, D), bf16),
            pltpu.VMEM((GROUPS, BLOCK, D), bf16),
            pltpu.VMEM((NZ - 1, BLOCK, D), bf16),
            pltpu.VMEM((BLOCK, D), f32),
            dma((SHARDS - 1,)), dma((SHARDS - 1,)),
            dma((6,)), dma((6,)),
            dma((4 * GROUPS,)), dma((4 * GROUPS,)),
            dma((10,)), dma((10,)),
            dma((GROUPS * (NX - 1),)), dma((GROUPS * (NX - 1),)),
            dma((GROUPS,)), dma((NZ - 1,)),
        ],
        compiler_params=pltpu.CompilerParams(
            collective_id=0, has_side_effects=True, vmem_limit_bytes=56 * 2**20
        ),
    )(pick, slots, live, rate, features, upstream, qkv, out, momentum)


def swap(bit, pair):
    def with_bit(number):
        return lambda p: lax.ppermute(
            p, "rep", [(i, i ^ 1 << number) for i in range(lax.axis_size("rep"))]
        )

    count = lax.axis_size("rep").bit_length() - 1
    return lax.switch(bit % count, [with_bit(n) for n in range(count)], pair)


def body(
    cell_features, upstream, qkv_weight, out_weight, momentum, key_tiles, live_blocks, step_index
):
    me = lax.axis_index("shard")
    lists = key_tiles[0].reshape(SHARDS, TILES * KB)
    owner, tile = lists // TILES, lists % TILES
    pick = jnp.minimum(jnp.sum(jnp.where(owner == me, tile, 0), axis=1), TILES - 1)
    away = (jnp.arange(SHARDS, dtype=jnp.int32)[:, None] - owner) % SHARDS
    slots = jnp.where(away == 0, tile, TILES - 1 + away)
    rate = jnp.float32(50.0) / (jnp.float32(500.0) + step_index.astype(jnp.float32))
    layer_out, pair, velocity = run_layer(
        pick, slots, live_blocks[0], rate.reshape(1),
        cell_features[0].reshape(TILES, TILE, D), upstream[0],
        qkv_weight[0], out_weight[0], momentum[0],
    )
    other = swap(step_index, pair).astype(jnp.float32)
    new_weight = (0.5 * (pair[0].astype(jnp.float32) + other[0])).astype(jnp.bfloat16)
    new_momentum = 0.5 * (velocity + other[1])
    return layer_out[None], new_weight[None], new_momentum[None]


def solution(mesh):
    rows = P("rep", "shard", None)
    placed = (rows, rows, rows, rows, rows, P("rep", None, None), P("rep", None), P())
    return jax.shard_map(
        body, mesh=mesh, in_specs=placed, out_specs=(rows, rows, rows), check_vma=False
    )
```

```python
import jax
import jax.numpy as jnp
from jax import lax
from jax.experimental import pallas as pl
from jax.experimental.pallas import tpu as pltpu
from jax.sharding import PartitionSpec as P

HEADS = 16
HEAD_DIM = 64
TILE = 128
KB = 6
TILES = 4
NX = 4
NZ = 4
SHARDS = NX * NZ
GROUPS = 4
D = 1024
GW = D // GROUPS
BLOCK = D // SHARDS
ROWS = TILES * TILE
SLOTS = TILES + SHARDS
MESH = pl.DeviceIdType.MESH

momentum_beta = 0.9


def at(z, x):
    return {"shard": z * NX + x}


def remote(ref, send, recv, device):
    return pltpu.make_async_remote_copy(
        src_ref=ref, dst_ref=ref, send_sem=send, recv_sem=recv, device_id=device, device_id_type=MESH
    )


def layer_kernel(
    pick_ref, slots_ref, live_ref, rate_ref, x_ref, up_ref, w_ref, ow_ref, mom_ref,
    layer_ref, pair_ref, vel_ref,
    below0, below1, below2, above0, above1, above2, packed, arrived, wbuf, owbuf, qbuf, kbuf, vbuf, att, grad, first, partial, second, total,
    cs, cr, ps, pr, zs, zr, ds, dr, es, er, gs, gr, hs, hr,
):
    me = lax.axis_index("shard")
    z, x = lax.div(me, NX), lax.rem(me, NX)
    right, left, far = (lax.rem(x + k, NX) for k in (1, NX - 1, NX // 2))
    ways = ((0, right, left), (1, left, right))

    barrier = pltpu.get_barrier_semaphore()
    for k in range(1, SHARDS):
        pl.semaphore_signal(
            barrier, 1, device_id={"shard": lax.rem(me + k, SHARDS)}, device_id_type=MESH
        )
    for g in range(GROUPS):
        for part in range(3):
            wbuf[g, z, x, :, pl.ds(part * GW, GW)] = w_ref[:, pl.ds(part * D + g * GW, GW)]
    owbuf[z, x] = ow_ref[...]
    pl.semaphore_wait(barrier, SHARDS - 1)

    def along_z(step, up, sending):
        came = z if sending else (z - 1 if up else z + 1)
        block = came - step if up else came + step
        valid = (block >= 0) & (block < NZ)
        if sending:
            valid &= (z < NZ - 1) if up else (z > 0)
        return valid, lax.rem(block + 2 * NZ, NZ), at(lax.rem(z + (1 if up else NZ - 1), NZ), x)

    items = [wbuf.at[g] for g in range(GROUPS)] + [owbuf]
    OUT = GROUPS

    def z_copy(i, step, up, sending):
        valid, block, to = along_z(step, up, sending)
        j = i * 6 + step * 2 + (0 if up else 1)
        return valid, block, remote(items[i].at[block, x], zs.at[j], zr.at[j], to)

    def x_copy(i, block, way, sending):
        _, to, back = ways[way]
        j = i * 8 + block * 2 + way
        return remote(items[i].at[block, x if sending else back], ds.at[j], dr.at[j], at(z, to))

    def far_copy(i, block, way, sending):
        _, to, back = ways[way]
        j = i * 8 + block * 2 + way
        half = pl.ds(way * (BLOCK // 2), BLOCK // 2)
        ref = items[i].at[block, back if sending else far, half]
        return remote(ref, es.at[j], er.at[j], at(z, to))

    def start_item(i):
        for up in (True, False):
            valid, _, c = z_copy(i, 0, up, True)
            pl.when(valid)(c.start)
        for way in range(2):
            x_copy(i, z, way, True).start()

    def relay_z(i, step):
        for up in (True, False):
            valid, block, c = z_copy(i, step, up, False)

            @pl.when(valid)
            def _():
                c.wait_recv()
                if step + 1 < NZ - 1:
                    more, _, onward = z_copy(i, step + 1, up, True)
                    pl.when(more)(onward.start)
                for way in range(2):
                    x_copy(i, block, way, True).start()

    def relay_x(i, *offsets):
        for offset in offsets:
            block = z + offset

            @pl.when((block >= 0) & (block < NZ))
            def _():
                inside = lax.rem(block + NZ, NZ)
                for way in range(2):
                    x_copy(i, inside, way, False).wait_recv()
                    far_copy(i, inside, way, True).start()

    def finish_item(i):
        for block in range(NZ):
            for way in range(2):
                far_copy(i, block, way, False).wait_recv()

    def drain_item(i):
        for step in range(NZ - 1):
            for up in (True, False):
                valid, _, c = z_copy(i, step, up, True)
                pl.when(valid)(c.wait_send)
        for block in range(NZ):
            for way in range(2):
                x_copy(i, block, way, True).wait_send()
                far_copy(i, block, way, True).wait_send()

    blocks = {0: x_ref, -1: below0, -2: below1, -3: below2, 1: above0, 2: above1, 3: above2}

    def column_copy(t, step, up, sending):
        valid, block, to = along_z(step, up, sending)
        sign = -1 if up else 1
        j = (step * 2 + (0 if up else 1)) * TILES + t
        return valid, block, pltpu.make_async_remote_copy(
            src_ref=blocks[sign * step].at[t], dst_ref=blocks[sign * (step + 1)].at[t],
            send_sem=cs.at[j], recv_sem=cr.at[j], device_id=to, device_id_type=MESH,
        )

    def tile_copy(block, away):
        j = (away - 1) * NZ + block
        return pltpu.make_async_remote_copy(
            src_ref=packed.at[away - 1, block], dst_ref=arrived.at[away - 1, block],
            send_sem=ps.at[j], recv_sem=pr.at[j],
            device_id=at(z, lax.rem(x + away, NX)), device_id_type=MESH,
        )

    def send_tiles(block, tiles):
        for away in (1, 3, 2):
            packed[away - 1, block] = tiles[pick_ref[block * NX + lax.rem(x + away, NX)]]
            tile_copy(block, away).start()

    def start_column():
        for t in range(TILES):
            for up in (True, False):
                valid, _, c = column_copy(t, 0, up, True)
                pl.when(valid)(c.start)

    def relay_column(step):
        for up in (True, False):
            valid, block, _ = column_copy(0, step, up, False)

            @pl.when(valid)
            def _():
                for t in range(TILES):
                    column_copy(t, step, up, False)[2].wait_recv()
                    if step + 1 < NZ - 1:
                        more, _, onward = column_copy(t, step + 1, up, True)
                        pl.when(more)(onward.start)
                send_tiles(block, blocks[(-1 if up else 1) * (step + 1)])

    groups = range(GROUPS)

    def each(act, *rest):
        for g in groups:
            act(g, *rest)

    each(start_item)
    send_tiles(z, x_ref)
    each(relay_z, 0)
    start_column()
    each(relay_z, 1)
    each(relay_x, 0)
    each(relay_z, 2)
    each(relay_x, -1, 1)
    relay_column(0)
    each(relay_x, -2, 2)
    relay_column(1)
    each(relay_x, -3, 3)
    each(finish_item)

    def project(slot, rows):
        count = rows.shape[0] // TILE

        def one(g, c):
            both = jnp.dot(
                rows, wbuf[g, :, :, :, GW : 3 * GW].reshape(D, 2 * GW),
                preferred_element_type=jnp.float32,
            ).astype(jnp.bfloat16).reshape(count, TILE, 2 * GW)
            kbuf[g, pl.ds(slot, count)] = both[:, :, 0:GW]
            vbuf[g, pl.ds(slot, count)] = both[:, :, GW : 2 * GW]
            return c

        lax.fori_loop(0, GROUPS, one, 0)

    def query(g, c):
        queries = jnp.dot(
            x_ref[...].reshape(ROWS, D), wbuf[g, :, :, :, 0:GW].reshape(D, GW),
            preferred_element_type=jnp.float32,
        ).astype(jnp.bfloat16)
        qbuf[g] = queries * jnp.bfloat16(HEAD_DIM ** -0.5)
        return c

    def project_block(*offsets):
        for offset in offsets:
            block = z + offset

            @pl.when((block >= 0) & (block < NZ))
            def _():
                inside = lax.rem(block + NZ, NZ)
                for away in range(1, NX):
                    tile_copy(inside, away).wait_recv()
                parts = [blocks[offset][pick_ref[inside * NX + x]]]
                parts += [arrived[away - 1, inside] for away in range(1, NX)]
                project(TILES + inside * NX, jnp.concatenate(parts, axis=0))

    lax.fori_loop(0, GROUPS, query, 0)
    project(0, x_ref[...].reshape(ROWS, D))
    project_block(0, -1, 1)
    relay_column(2)
    start_item(OUT)
    project_block(-2, 2, -3, 3)
    relay_z(OUT, 0)

    lane_head = lax.broadcasted_iota(jnp.int32, (TILE, GW), 1) // HEAD_DIM
    slot_of = lax.broadcasted_iota(jnp.int32, (1, KB * TILE), 1) // TILE
    nt = (((1,), (1,)), ((), ()))
    tn = (((0,), (0,)), ((), ()))

    def first_copy(g, step):
        to = lax.rem(x + step, NX)
        i = g * (NX - 1) + step - 1
        return pltpu.make_async_remote_copy(
            src_ref=grad.at[g, to], dst_ref=first.at[g, step - 1],
            send_sem=gs.at[i], recv_sem=gr.at[i],
            device_id=at(z, to), device_id_type=MESH,
        )

    def second_copy(g, slot):
        return pltpu.make_async_remote_copy(
            src_ref=partial.at[g], dst_ref=second.at[slot],
            send_sem=hs.at[g], recv_sem=hr.at[slot],
            device_id=at(g, x), device_id_type=MESH,
        )

    def finish_first(g):
        summed = grad[g, x].astype(jnp.float32)
        for step in range(1, NX):
            first_copy(g, step).wait_recv()
            summed += first[g, step - 1].astype(jnp.float32)

        @pl.when(z == g)
        def _():
            total[...] = summed

        @pl.when(z != g)
        def _():
            partial[g] = summed.astype(jnp.bfloat16)
            second_copy(g, lax.rem(z - g + NZ, NZ) - 1).start()

    def group(g):
        def attend(i, c):
            live = live_ref[me * TILES + i]
            keys, values = [], []
            for j in range(KB):
                slot = slots_ref[i * KB + j]
                keys.append(kbuf[g, slot])
                values.append(vbuf[g, slot])
            q = qbuf[g, pl.ds(pl.multiple_of(i * TILE, TILE), TILE), :]
            masked = jnp.concatenate(
                [jnp.where(lane_head == h, q, jnp.bfloat16(0)) for h in range(GW // HEAD_DIM)], axis=0
            )
            scores = lax.dot_general(
                masked, jnp.concatenate(keys, axis=0), nt, preferred_element_type=jnp.float32
            )
            scores = jnp.where(slot_of < live, scores, jnp.float32(-1e30))
            exponent = jnp.exp(scores - jnp.max(scores, axis=1, keepdims=True))
            scale = 1.0 / jnp.sum(exponent, axis=1, keepdims=True)
            mixed = jnp.dot(
                exponent.astype(jnp.bfloat16), jnp.concatenate(values, axis=0),
                preferred_element_type=jnp.float32,
            ) * scale
            joined = jnp.zeros((TILE, GW), jnp.float32)
            for h in range(GW // HEAD_DIM):
                joined = jnp.where(lane_head == h, mixed[h * TILE : (h + 1) * TILE], joined)
            att[g, pl.ds(pl.multiple_of(i * TILE, TILE), TILE), :] = joined.astype(jnp.bfloat16)
            return c

        lax.fori_loop(0, TILES, attend, 0)
        grad[g] = (
            lax.dot_general(att[g], up_ref[...], tn, preferred_element_type=jnp.float32)
            .astype(jnp.bfloat16)
            .reshape(NX, BLOCK, D)
        )
        for step in range(1, NX):
            first_copy(g, step).start()
        if g > 0:
            finish_first(g - 1)

    group(0)
    relay_z(OUT, 1)
    relay_x(OUT, 0)
    group(1)
    relay_z(OUT, 2)
    relay_x(OUT, -1, 1)
    group(2)
    relay_x(OUT, -2, 2, -3, 3)
    group(3)
    finish_item(OUT)

    def project_out(i, c):
        rows = pl.ds(pl.multiple_of(i * TILE, TILE), TILE)
        product = x_ref[i].astype(jnp.float32)
        for g in groups:
            product += jnp.dot(
                att[g, rows, :], owbuf[g].reshape(GW, D), preferred_element_type=jnp.float32
            )
        layer_ref[rows, :] = product.astype(jnp.bfloat16)
        return c

    lax.fori_loop(0, TILES // 2, project_out, 0)
    finish_first(GROUPS - 1)
    lax.fori_loop(TILES // 2, TILES, project_out, 0)

    summed = total[...]
    for slot in range(NZ - 1):
        second_copy(0, slot).wait_recv()
        summed += second[slot].astype(jnp.float32)
    velocity = momentum_beta * mom_ref[...] + summed
    stepped = ow_ref[...].astype(jnp.float32) - rate_ref[0] * velocity
    vel_ref[...] = velocity
    pair_ref[0] = stepped.astype(jnp.bfloat16)
    pair_ref[1] = velocity.astype(jnp.bfloat16)

    for i in range(GROUPS + 1):
        drain_item(i)
    for step in range(NZ - 1):
        for up in (True, False):
            for t in range(TILES):
                valid, _, c = column_copy(t, step, up, True)
                pl.when(valid)(c.wait_send)
    for block in range(NZ):
        for away in range(1, NX):
            tile_copy(block, away).wait_send()
    for g in groups:
        for step in range(1, NX):
            first_copy(g, step).wait_send()

        @pl.when(z != g)
        def _():
            second_copy(g, 0).wait_send()


def run_layer(pick, slots, live, rate, features, upstream, qkv, out, momentum):
    vmem = pl.BlockSpec(memory_space=pltpu.VMEM)
    smem = pl.BlockSpec(memory_space=pltpu.SMEM)
    bf16, f32 = jnp.bfloat16, jnp.float32

    def sems(count):
        return [pltpu.SemaphoreType.DMA((count,))] * 2

    return pl.pallas_call(
        layer_kernel,
        name="layer",
        out_shape=(
            jax.ShapeDtypeStruct((ROWS, D), bf16),
            jax.ShapeDtypeStruct((2, BLOCK, D), bf16),
            jax.ShapeDtypeStruct((BLOCK, D), f32),
        ),
        in_specs=[smem] * 4 + [vmem] * 5,
        out_specs=(vmem, vmem, vmem),
        scratch_shapes=[
            *[pltpu.VMEM((TILES, TILE, D), bf16)] * 6,
            pltpu.VMEM((NX - 1, NZ, TILE, D), bf16),
            pltpu.VMEM((NX - 1, NZ, TILE, D), bf16),
            pltpu.VMEM((GROUPS, NZ, NX, BLOCK, 3 * GW), bf16),
            pltpu.VMEM((NZ, NX, BLOCK, D), bf16),
            pltpu.VMEM((GROUPS, ROWS, GW), bf16),
            pltpu.VMEM((GROUPS, SLOTS, TILE, GW), bf16),
            pltpu.VMEM((GROUPS, SLOTS, TILE, GW), bf16),
            pltpu.VMEM((GROUPS, ROWS, GW), bf16),
            pltpu.VMEM((GROUPS, NX, BLOCK, D), bf16),
            pltpu.VMEM((GROUPS, NX - 1, BLOCK, D), bf16),
            pltpu.VMEM((GROUPS, BLOCK, D), bf16),
            pltpu.VMEM((NZ - 1, BLOCK, D), bf16),
            pltpu.VMEM((BLOCK, D), f32),
            *sems(6 * TILES), *sems((NX - 1) * NZ),
            *sems(6 * (GROUPS + 1)), *sems(8 * (GROUPS + 1)), *sems(8 * (GROUPS + 1)),
            *sems(GROUPS * (NX - 1)),
            pltpu.SemaphoreType.DMA((GROUPS,)), pltpu.SemaphoreType.DMA((NZ - 1,)),
        ],
        compiler_params=pltpu.CompilerParams(
            collective_id=0, has_side_effects=True, vmem_limit_bytes=58 * 2**20
        ),
    )(pick, slots, live, rate, features, upstream, qkv, out, momentum)


def swap(bit, pair):
    def with_bit(number):
        return lambda p: lax.ppermute(
            p, "rep", [(i, i ^ 1 << number) for i in range(lax.axis_size("rep"))]
        )

    count = lax.axis_size("rep").bit_length() - 1
    return lax.switch(bit % count, [with_bit(n) for n in range(count)], pair)


def body(
    cell_features, upstream, qkv_weight, out_weight, momentum, key_tiles, live_blocks, step_index
):
    me = lax.axis_index("shard")
    z, x = me // NX, me % NX
    lists = key_tiles[0].reshape(NZ, NX, TILES * KB)
    row = lax.dynamic_index_in_dim(lists, z, 0, keepdims=False)
    owners = jnp.arange(NZ, dtype=jnp.int32)[:, None, None] * NX + x
    pick = jnp.sum(jnp.where(row[None] // TILES == owners, row[None] % TILES, 0), axis=2)
    pick = jnp.minimum(pick, TILES - 1).reshape(-1)
    mine = lax.dynamic_index_in_dim(row, x, 0, keepdims=False)
    owner, tile = mine // TILES, mine % TILES
    slots = jnp.where(
        owner == me, tile, TILES + owner // NX * NX + (x - owner % NX) % NX
    )
    rate = jnp.float32(50.0) / (jnp.float32(500.0) + step_index.astype(jnp.float32))
    layer_out, pair, velocity = run_layer(
        pick, slots, live_blocks[0], rate.reshape(1),
        cell_features[0].reshape(TILES, TILE, D), upstream[0],
        qkv_weight[0], out_weight[0], momentum[0],
    )
    other = swap(step_index, pair).astype(jnp.float32)
    new_weight = (0.5 * (pair[0].astype(jnp.float32) + other[0])).astype(jnp.bfloat16)
    new_momentum = 0.5 * (velocity + other[1])
    return layer_out[None], new_weight[None], new_momentum[None]


def solution(mesh):
    rows = P("rep", "shard", None)
    placed = (rows, rows, rows, rows, rows, P("rep", None, None), P("rep", None), P())
    return jax.shard_map(
        body, mesh=mesh, in_specs=placed, out_specs=(rows, rows, rows), check_vma=False
    )
```

```python
import jax
import jax.numpy as jnp
from jax import lax
from jax.experimental import pallas as pl
from jax.experimental.pallas import tpu as pltpu
from jax.sharding import PartitionSpec as P

HEADS = 16
HEAD_DIM = 64
TILE = 128
KB = 6
TILES = 4
NX = 4
NZ = 4
SHARDS = NX * NZ
GROUPS = NZ
D = 1024
GW = D // GROUPS
BLOCK = D // SHARDS
ROWS = TILES * TILE
MESH = pl.DeviceIdType.MESH

momentum_beta = 0.9


def at(z, x):
    return {"shard": z * NX + x}


def remote(src, dst, send, recv, device):
    return pltpu.make_async_remote_copy(
        src_ref=src, dst_ref=dst, send_sem=send, recv_sem=recv, device_id=device, device_id_type=MESH
    )


def layer_kernel(
    lists_ref, live_ref, step_ref, x_ref, up_ref, w_ref, ow_ref, mom_ref,
    layer_ref, pair_ref, vel_ref,
    below0, below1, below2, above0, above1, above2,
    wparts, wbuf, owbuf, qbuf, kbuf, vbuf, mixed_out, att, grad, first, partial, second, total,
    cs, cr, ws, wr, zs, zr, ds, dr, es, er, as_, ar, gs, gr, hs, hr,
):
    me = lax.axis_index("shard")
    z, x = lax.div(me, NX), lax.rem(me, NX)
    right, left, far = (lax.rem(x + k, NX) for k in (1, NX - 1, NX // 2))
    ways = ((0, right, left), (1, left, right))

    def behind(away):
        return lax.rem(z - away + NZ, NZ)

    def ahead(away):
        return lax.rem(z + away, NZ)

    barrier = pltpu.get_barrier_semaphore()
    for k in range(1, SHARDS):
        pl.semaphore_signal(
            barrier, 1, device_id={"shard": lax.rem(me + k, SHARDS)}, device_id_type=MESH
        )
    for g in range(GROUPS):
        for part in range(3):
            wparts[g, :, pl.ds(part * GW, GW)] = w_ref[:, pl.ds(part * D + g * GW, GW)]
    wbuf[z, x] = wparts[z]
    owbuf[z, x] = ow_ref[...]
    pl.semaphore_wait(barrier, SHARDS - 1)

    def along_z(step, up, sending):
        came = z if sending else (z - 1 if up else z + 1)
        block = came - step if up else came + step
        valid = (block >= 0) & (block < NZ)
        if sending:
            valid &= (z < NZ - 1) if up else (z > 0)
        return valid, lax.rem(block + 2 * NZ, NZ), at(lax.rem(z + (1 if up else NZ - 1), NZ), x)

    W, OUT, K, V = range(4)

    def view(item, block, column, half=None):
        if item in (W, OUT):
            ref = (wbuf if item == W else owbuf).at[block, column]
            return ref if half is None else ref.at[pl.ds(half * (BLOCK // 2), BLOCK // 2)]
        base = (block * NX + column) * TILES
        ref = kbuf if item == K else vbuf
        if half is None:
            return ref.at[pl.ds(base, TILES)]
        return ref.at[pl.ds(base + half * (TILES // 2), TILES // 2)]

    def x_copy(item, block, way, sending):
        _, to, back = ways[way]
        j = item * 8 + block * 2 + way
        ref = view(item, block, x if sending else back)
        return remote(ref, ref, ds.at[j], dr.at[j], at(z, to))

    def far_copy(item, block, way, sending):
        _, to, back = ways[way]
        j = item * 8 + block * 2 + way
        ref = view(item, block, back if sending else far, way)
        return remote(ref, ref, es.at[j], er.at[j], at(z, to))

    def share_x(item, block):
        for way in range(2):
            x_copy(item, block, way, True).start()

    def relay_x(item, block):
        for way in range(2):
            x_copy(item, block, way, False).wait_recv()
            far_copy(item, block, way, True).start()

    def finish_x(item):
        for block in range(NZ):
            for way in range(2):
                far_copy(item, block, way, False).wait_recv()

    def at_offset(offset, act):
        block = z + offset

        @pl.when((block >= 0) & (block < NZ))
        def _():
            act(lax.rem(block + NZ, NZ))

    def weight_copy(away, sending):
        to = ahead(away)
        return remote(
            wparts.at[to], wbuf.at[z if sending else behind(away), x],
            ws.at[away - 1], wr.at[away - 1], at(to, x),
        )

    blocks = {0: x_ref, -1: below0, -2: below1, -3: below2, 1: above0, 2: above1, 3: above2}

    def column_copy(t, step, up, sending):
        valid, _, to = along_z(step, up, sending)
        sign = -1 if up else 1
        j = (step * 2 + (0 if up else 1)) * TILES + t
        return valid, remote(
            blocks[sign * step].at[t], blocks[sign * (step + 1)].at[t], cs.at[j], cr.at[j], to
        )

    def start_column():
        for t in range(TILES):
            for up in (True, False):
                valid, c = column_copy(t, 0, up, True)
                pl.when(valid)(c.start)

    def relay_column(step):
        for up in (True, False):
            valid, _ = column_copy(0, step, up, False)

            @pl.when(valid)
            def _():
                for t in range(TILES):
                    column_copy(t, step, up, False)[1].wait_recv()
                    if step + 1 < NZ - 1:
                        more, onward = column_copy(t, step + 1, up, True)
                        pl.when(more)(onward.start)

    def out_copy(step, up, sending):
        valid, block, to = along_z(step, up, sending)
        j = step * 2 + (0 if up else 1)
        ref = owbuf.at[block, x]
        return valid, block, remote(ref, ref, zs.at[j], zr.at[j], to)

    def start_out():
        for up in (True, False):
            valid, _, c = out_copy(0, up, True)
            pl.when(valid)(c.start)
        share_x(OUT, z)

    def relay_out(step):
        for up in (True, False):
            valid, block, c = out_copy(step, up, False)

            @pl.when(valid)
            def _():
                c.wait_recv()
                if step + 1 < NZ - 1:
                    more, _, onward = out_copy(step + 1, up, True)
                    pl.when(more)(onward.start)
                share_x(OUT, block)

    def project(block, rows):
        whole = jnp.dot(
            rows[...].reshape(ROWS, D), wbuf[...].reshape(D, 3 * GW),
            preferred_element_type=jnp.float32,
        ).astype(jnp.bfloat16).reshape(TILES, TILE, 3 * GW)
        base = pl.ds((block * NX + x) * TILES, TILES)
        kbuf[base] = whole[:, :, GW : 2 * GW]
        vbuf[base] = whole[:, :, 2 * GW :]
        share_x(K, block)
        share_x(V, block)
        qbuf[block] = whole[:, :, 0:GW] * jnp.bfloat16(HEAD_DIM ** -0.5)

    def project_at(offset):
        at_offset(offset, lambda block: project(block, blocks[offset]))

    def relay_keys(offset):
        def act(block):
            relay_x(K, block)
            relay_x(V, block)

        at_offset(offset, act)

    for away in (1, 3, 2):
        weight_copy(away, True).start()
    share_x(W, z)
    start_column()
    for away in (1, 3, 2):
        weight_copy(away, False).wait_recv()
        share_x(W, behind(away))
    for away in (0, 1, 3, 2):
        relay_x(W, behind(away))
    finish_x(W)

    project(z, x_ref)
    relay_column(0)
    project_at(-1)
    project_at(1)
    relay_keys(0)
    relay_column(1)
    project_at(-2)
    project_at(2)
    relay_keys(-1)
    relay_keys(1)
    relay_column(2)
    project_at(-3)
    project_at(3)
    start_out()
    for offset in (-2, 2, -3, 3):
        relay_keys(offset)
    finish_x(K)
    finish_x(V)

    lane_head = lax.broadcasted_iota(jnp.int32, (TILE, GW), 1) // HEAD_DIM
    slot_of = lax.broadcasted_iota(jnp.int32, (1, KB * TILE), 1) // TILE
    nt = (((1,), (1,)), ((), ()))
    tn = (((0,), (0,)), ((), ()))

    def mixed_copy(away, sending):
        return remote(
            mixed_out.at[away - 1], att.at[z if sending else behind(away)],
            as_.at[away - 1], ar.at[away - 1], at(ahead(away), x),
        )

    def attend(away):
        block = ahead(away)

        def one(i, c):
            tile = (block * NX + x) * TILES + i
            live = live_ref[tile]
            keys, values = [], []
            for j in range(KB):
                listed = lists_ref[tile, j]
                keys.append(kbuf[listed])
                values.append(vbuf[listed])
            q = qbuf[block, i]
            masked = jnp.concatenate(
                [jnp.where(lane_head == h, q, jnp.bfloat16(0)) for h in range(GW // HEAD_DIM)], axis=0
            )
            scores = lax.dot_general(
                masked, jnp.concatenate(keys, axis=0), nt, preferred_element_type=jnp.float32
            )
            scores = jnp.where(slot_of < live, scores, jnp.float32(-1e30))
            exponent = jnp.exp(scores - jnp.max(scores, axis=1, keepdims=True))
            scale = 1.0 / jnp.sum(exponent, axis=1, keepdims=True)
            mixed = jnp.dot(
                exponent.astype(jnp.bfloat16), jnp.concatenate(values, axis=0),
                preferred_element_type=jnp.float32,
            ) * scale
            joined = jnp.zeros((TILE, GW), jnp.float32)
            for h in range(GW // HEAD_DIM):
                joined = jnp.where(lane_head == h, mixed[h * TILE : (h + 1) * TILE], joined)
            joined = joined.astype(jnp.bfloat16)
            if away:
                mixed_out[away - 1, i] = joined
            else:
                att[z, i] = joined
            return c

        lax.fori_loop(0, TILES, one, 0)
        if away:
            mixed_copy(away, True).start()

    def first_copy(away, step):
        to = lax.rem(x + step, NX)
        i = away * (NX - 1) + step - 1
        return remote(
            grad.at[away, to], first.at[away, step - 1], gs.at[i], gr.at[i], at(z, to)
        )

    def second_copy(away):
        return remote(
            partial.at[away - 1], second.at[away - 1],
            hs.at[away - 1], hr.at[away - 1], at(behind(away), x),
        )

    def gradient(away):
        if away:
            mixed_copy(away, False).wait_recv()
        grad[away] = (
            lax.dot_general(
                att[behind(away)].reshape(ROWS, GW), up_ref[...], tn,
                preferred_element_type=jnp.float32,
            )
            .astype(jnp.bfloat16)
            .reshape(NX, BLOCK, D)
        )
        for step in range(1, NX):
            first_copy(away, step).start()

    def finish_first(away):
        summed = grad[away, x].astype(jnp.float32)
        for step in range(1, NX):
            first_copy(away, step).wait_recv()
            summed += first[away, step - 1].astype(jnp.float32)
        if away:
            partial[away - 1] = summed.astype(jnp.bfloat16)
            second_copy(away).start()
        else:
            total[...] = summed

    attend(2)
    relay_out(0)
    relay_x(OUT, z)
    attend(1)
    relay_out(1)
    gradient(2)
    attend(3)
    relay_out(2)
    gradient(1)
    finish_first(2)
    for offset in (-1, 1):
        at_offset(offset, lambda block: relay_x(OUT, block))
    attend(0)
    gradient(3)
    finish_first(1)
    gradient(0)
    for offset in (-2, 2, -3, 3):
        at_offset(offset, lambda block: relay_x(OUT, block))
    finish_first(3)

    def project_out(i, c):
        product = x_ref[i].astype(jnp.float32)
        for g in range(GROUPS):
            product += jnp.dot(
                att[g, i], owbuf[g].reshape(GW, D), preferred_element_type=jnp.float32
            )
        layer_ref[pl.ds(pl.multiple_of(i * TILE, TILE), TILE), :] = product.astype(jnp.bfloat16)
        return c

    finish_x(OUT)
    lax.fori_loop(0, TILES // 2, project_out, 0)
    finish_first(0)
    lax.fori_loop(TILES // 2, TILES, project_out, 0)

    summed = total[...]
    for away in range(1, NZ):
        second_copy(away).wait_recv()
        summed += second[away - 1].astype(jnp.float32)
    velocity = momentum_beta * mom_ref[...] + summed
    rate = 50.0 / (500.0 + jnp.full((BLOCK, D), step_ref[0].astype(jnp.float32)))
    stepped = ow_ref[...].astype(jnp.float32) - rate * velocity
    vel_ref[...] = velocity
    pair_ref[0] = stepped.astype(jnp.bfloat16)
    pair_ref[1] = velocity.astype(jnp.bfloat16)

    for item in range(4):
        for block in range(NZ):
            for way in range(2):
                x_copy(item, block, way, True).wait_send()
                far_copy(item, block, way, True).wait_send()
    for step in range(NZ - 1):
        for up in (True, False):
            valid, _, c = out_copy(step, up, True)
            pl.when(valid)(c.wait_send)
            for t in range(TILES):
                valid, c = column_copy(t, step, up, True)
                pl.when(valid)(c.wait_send)
    for away in range(1, NZ):
        weight_copy(away, True).wait_send()
        mixed_copy(away, True).wait_send()
        second_copy(away).wait_send()
    for away in range(NZ):
        for step in range(1, NX):
            first_copy(away, step).wait_send()


def run_layer(lists, live, step, features, upstream, qkv, out, momentum):
    vmem = pl.BlockSpec(memory_space=pltpu.VMEM)
    smem = pl.BlockSpec(memory_space=pltpu.SMEM)
    bf16, f32 = jnp.bfloat16, jnp.float32

    def sems(count):
        return [pltpu.SemaphoreType.DMA((count,))] * 2

    return pl.pallas_call(
        layer_kernel,
        name="layer",
        out_shape=(
            jax.ShapeDtypeStruct((ROWS, D), bf16),
            jax.ShapeDtypeStruct((2, BLOCK, D), bf16),
            jax.ShapeDtypeStruct((BLOCK, D), f32),
        ),
        in_specs=[smem] * 3 + [vmem] * 5,
        out_specs=(vmem, vmem, vmem),
        scratch_shapes=[
            *[pltpu.VMEM((TILES, TILE, D), bf16)] * 6,
            pltpu.VMEM((GROUPS, BLOCK, 3 * GW), bf16),
            pltpu.VMEM((NZ, NX, BLOCK, 3 * GW), bf16),
            pltpu.VMEM((NZ, NX, BLOCK, D), bf16),
            pltpu.VMEM((NZ, TILES, TILE, GW), bf16),
            pltpu.VMEM((SHARDS * TILES, TILE, GW), bf16),
            pltpu.VMEM((SHARDS * TILES, TILE, GW), bf16),
            pltpu.VMEM((NZ - 1, TILES, TILE, GW), bf16),
            pltpu.VMEM((GROUPS, TILES, TILE, GW), bf16),
            pltpu.VMEM((GROUPS, NX, BLOCK, D), bf16),
            pltpu.VMEM((GROUPS, NX - 1, BLOCK, D), bf16),
            pltpu.VMEM((NZ - 1, BLOCK, D), bf16),
            pltpu.VMEM((NZ - 1, BLOCK, D), bf16),
            pltpu.VMEM((BLOCK, D), f32),
            *sems(6 * TILES), *sems(NZ - 1), *sems(6), *sems(8 * 4), *sems(8 * 4),
            *sems(NZ - 1), *sems(GROUPS * (NX - 1)), *sems(NZ - 1),
        ],
        compiler_params=pltpu.CompilerParams(
            collective_id=0, has_side_effects=True, vmem_limit_bytes=58 * 2**20
        ),
    )(lists, live, step, features, upstream, qkv, out, momentum)


def swap(bit, pair):
    def with_bit(number):
        return lambda p: lax.ppermute(
            p, "rep", [(i, i ^ 1 << number) for i in range(lax.axis_size("rep"))]
        )

    count = lax.axis_size("rep").bit_length() - 1
    return lax.switch(bit % count, [with_bit(n) for n in range(count)], pair)


def body(
    cell_features, upstream, qkv_weight, out_weight, momentum, key_tiles, live_blocks, step_index
):
    layer_out, pair, velocity = run_layer(
        key_tiles[0], live_blocks[0], step_index.reshape(1),
        cell_features[0].reshape(TILES, TILE, D), upstream[0],
        qkv_weight[0], out_weight[0], momentum[0],
    )
    other = swap(step_index, pair).astype(jnp.float32)
    new_weight = (0.5 * (pair[0].astype(jnp.float32) + other[0])).astype(jnp.bfloat16)
    new_momentum = 0.5 * (velocity + other[1])
    return layer_out[None], new_weight[None], new_momentum[None]


def solution(mesh):
    rows = P("rep", "shard", None)
    placed = (rows, rows, rows, rows, rows, P("rep", None, None), P("rep", None), P())
    return jax.shard_map(
        body, mesh=mesh, in_specs=placed, out_specs=(rows, rows, rows), check_vma=False
    )
```

```python
import functools

import jax
import jax.numpy as jnp
from jax import lax
from jax.experimental import pallas as pl
from jax.experimental.pallas import tpu as pltpu
from jax.sharding import PartitionSpec as P

HEADS = 16
HEAD_DIM = 64
TILE = 128
KB = 6
TILES = 4
NX = 4
NZ = 4
SHARDS = NX * NZ
GROUPS = NZ
D = 1024
GW = D // GROUPS
BLOCK = D // SHARDS
ROWS = TILES * TILE
MESH = pl.DeviceIdType.MESH

momentum_beta = 0.9


def at(z, x):
    return {"shard": z * NX + x}


def remote(src, dst, send, recv, device):
    return pltpu.make_async_remote_copy(
        src_ref=src, dst_ref=dst, send_sem=send, recv_sem=recv, device_id=device, device_id_type=MESH
    )


def layer_kernel(
    lists_ref, live_ref, step_ref, x_ref, up_ref, w_ref, ow_ref, mom_ref,
    layer_ref, pair_ref, vel_ref,
    below0, below1, below2, above0, above1, above2,
    wparts, wbuf, owbuf, qbuf, kvbuf, mixed_out, att, grad, first, partial, second, total,
    cs, cr, ws, wr, zs, zr, ds, dr, es, er, as_, ar, gs, gr, hs, hr,
):
    me = lax.axis_index("shard")
    z, x = lax.div(me, NX), lax.rem(me, NX)
    right, left, far = (lax.rem(x + k, NX) for k in (1, NX - 1, NX // 2))
    ways = ((0, right, left), (1, left, right))

    def behind(away):
        return lax.rem(z - away + NZ, NZ)

    def ahead(away):
        return lax.rem(z + away, NZ)

    barrier = pltpu.get_barrier_semaphore()
    peers = [at(z, lax.rem(x + k, NX)) for k in range(1, NX)]
    peers += [at(lax.rem(z + k, NZ), x) for k in range(1, NZ)]
    for peer in peers:
        pl.semaphore_signal(barrier, 1, device_id=peer, device_id_type=MESH)
    for g in range(GROUPS):
        for part in range(3):
            wparts[g, :, pl.ds(part * GW, GW)] = w_ref[:, pl.ds(part * D + g * GW, GW)]
    wbuf[z, x] = wparts[z]
    owbuf[z, x] = ow_ref[...]
    pl.semaphore_wait(barrier, len(peers))

    def along_z(step, up, sending):
        came = z if sending else (z - 1 if up else z + 1)
        block = came - step if up else came + step
        valid = (block >= 0) & (block < NZ)
        if sending:
            valid &= (z < NZ - 1) if up else (z > 0)
        return valid, lax.rem(block + 2 * NZ, NZ), at(lax.rem(z + (1 if up else NZ - 1), NZ), x)

    W, OUT, PAIRS = 0, 1, (2, 3)

    def view(item, block, column, half=None):
        if item in PAIRS:
            base = (block * NX + column) * TILES + (item - PAIRS[0]) * 2
            return kvbuf.at[pl.ds(base, 2)] if half is None else kvbuf.at[pl.ds(base + half, 1)]
        ref = (wbuf if item == W else owbuf).at[block, column]
        return ref if half is None else ref.at[pl.ds(half * (BLOCK // 2), BLOCK // 2)]

    def x_copy(item, block, way, sending):
        _, to, back = ways[way]
        j = item * 8 + block * 2 + way
        ref = view(item, block, x if sending else back)
        return remote(ref, ref, ds.at[j], dr.at[j], at(z, to))

    def far_copy(item, block, way, sending):
        _, to, back = ways[way]
        j = item * 8 + block * 2 + way
        ref = view(item, block, back if sending else far, way)
        return remote(ref, ref, es.at[j], er.at[j], at(z, to))

    def share_x(item, block):
        for way in range(2):
            x_copy(item, block, way, True).start()

    def relay_x(item, block):
        for way in range(2):
            x_copy(item, block, way, False).wait_recv()
            far_copy(item, block, way, True).start()

    def finish_x(item):
        for block in range(NZ):
            for way in range(2):
                far_copy(item, block, way, False).wait_recv()

    def at_offset(offset, act):
        block = z + offset

        @pl.when((block >= 0) & (block < NZ))
        def _():
            act(lax.rem(block + NZ, NZ))

    def weight_copy(away, sending):
        to = ahead(away)
        return remote(
            wparts.at[to], wbuf.at[z if sending else behind(away), x],
            ws.at[away - 1], wr.at[away - 1], at(to, x),
        )

    blocks = {0: x_ref, -1: below0, -2: below1, -3: below2, 1: above0, 2: above1, 3: above2}

    def column_copy(t, step, up, sending):
        valid, _, to = along_z(step, up, sending)
        sign = -1 if up else 1
        j = (step * 2 + (0 if up else 1)) * TILES + t
        return valid, remote(
            blocks[sign * step].at[t], blocks[sign * (step + 1)].at[t], cs.at[j], cr.at[j], to
        )

    def start_column(t):
        for up in (True, False):
            valid, c = column_copy(t, 0, up, True)
            pl.when(valid)(c.start)

    def relay_column(t, step):
        for up in (True, False):
            valid, c = column_copy(t, step, up, False)

            @pl.when(valid)
            def _():
                c.wait_recv()
                if step + 1 < NZ - 1:
                    more, onward = column_copy(t, step + 1, up, True)
                    pl.when(more)(onward.start)

    def out_copy(step, up, sending):
        valid, block, to = along_z(step, up, sending)
        j = step * 2 + (0 if up else 1)
        ref = owbuf.at[block, x]
        return valid, block, remote(ref, ref, zs.at[j], zr.at[j], to)

    def start_out():
        for up in (True, False):
            valid, _, c = out_copy(0, up, True)
            pl.when(valid)(c.start)

    def relay_out(step):
        for up in (True, False):
            valid, block, c = out_copy(step, up, False)

            @pl.when(valid)
            def _():
                c.wait_recv()
                if step + 1 < NZ - 1:
                    more, _, onward = out_copy(step + 1, up, True)
                    pl.when(more)(onward.start)
                share_x(OUT, block)

    def project(pair, block, rows):
        whole = jnp.dot(
            rows[pl.ds(pair * 2, 2)].reshape(2 * TILE, D), wbuf[...].reshape(D, 3 * GW),
            preferred_element_type=jnp.float32,
        ).astype(jnp.bfloat16).reshape(2, TILE, 3 * GW)
        base = pl.ds((block * NX + x) * TILES + pair * 2, 2)
        kvbuf[base, 0] = whole[:, :, GW : 2 * GW]
        kvbuf[base, 1] = whole[:, :, 2 * GW :]
        share_x(PAIRS[pair], block)
        qbuf[block, pl.ds(pair * 2, 2)] = whole[:, :, 0:GW] * jnp.bfloat16(HEAD_DIM ** -0.5)

    def both(distance, act):
        for offset in (-distance, distance):
            at_offset(offset, functools.partial(act, offset))

    def project_at(distance, pair):
        both(distance, lambda offset, block: project(pair, block, blocks[offset]))

    def relay_keys(distance, pair):
        both(distance, lambda offset, block: relay_x(PAIRS[pair], block))

    def relay_out_x(distance):
        both(distance, lambda offset, block: relay_x(OUT, block))

    start_column(0)
    for away in (1, 3, 2):
        weight_copy(away, True).start()
    share_x(W, z)
    start_column(1)
    for away in (1, 3, 2):
        weight_copy(away, False).wait_recv()
        share_x(W, behind(away))
    start_column(2)
    share_x(OUT, z)
    for away in (0, 1, 3, 2):
        relay_x(W, behind(away))
    start_column(3)
    finish_x(W)

    project(0, z, x_ref)
    relay_column(0, 0)
    project(1, z, x_ref)
    relay_x(PAIRS[0], z)
    relay_column(1, 0)
    project_at(1, 0)
    relay_x(PAIRS[1], z)
    relay_column(2, 0)
    relay_column(3, 0)
    project_at(1, 1)
    relay_column(0, 1)
    relay_keys(1, 0)
    relay_column(1, 1)
    project_at(2, 0)
    relay_keys(1, 1)
    relay_column(2, 1)
    relay_column(3, 1)
    project_at(2, 1)
    relay_keys(2, 0)
    relay_column(0, 2)
    relay_column(1, 2)
    start_out()
    project_at(3, 0)
    relay_keys(2, 1)
    relay_column(2, 2)
    relay_column(3, 2)
    project_at(3, 1)
    relay_out(0)
    relay_x(OUT, z)
    relay_keys(3, 0)
    relay_keys(3, 1)
    relay_out(1)
    for pair in PAIRS:
        finish_x(pair)

    lane_head = lax.broadcasted_iota(jnp.int32, (TILE, GW), 1) // HEAD_DIM
    slot_of = lax.broadcasted_iota(jnp.int32, (1, KB * TILE), 1) // TILE
    nt = (((1,), (1,)), ((), ()))
    tn = (((0,), (0,)), ((), ()))

    def mixed_copy(away, sending):
        return remote(
            mixed_out.at[away - 1], att.at[z if sending else behind(away)],
            as_.at[away - 1], ar.at[away - 1], at(ahead(away), x),
        )

    def attend(away):
        block = ahead(away)

        def one(i, c):
            tile = (block * NX + x) * TILES + i
            live = live_ref[tile]
            keys, values = [], []
            for j in range(KB):
                listed = lists_ref[tile, j]
                keys.append(kvbuf[listed, 0])
                values.append(kvbuf[listed, 1])
            q = qbuf[block, i]
            masked = jnp.concatenate(
                [jnp.where(lane_head == h, q, jnp.bfloat16(0)) for h in range(GW // HEAD_DIM)], axis=0
            )
            scores = lax.dot_general(
                masked, jnp.concatenate(keys, axis=0), nt, preferred_element_type=jnp.float32
            )
            scores = jnp.where(slot_of < live, scores, jnp.float32(-1e30))
            exponent = jnp.exp(scores - jnp.max(scores, axis=1, keepdims=True))
            scale = 1.0 / jnp.sum(exponent, axis=1, keepdims=True)
            mixed = jnp.dot(
                exponent.astype(jnp.bfloat16), jnp.concatenate(values, axis=0),
                preferred_element_type=jnp.float32,
            ) * scale
            joined = jnp.zeros((TILE, GW), jnp.float32)
            for h in range(GW // HEAD_DIM):
                joined = jnp.where(lane_head == h, mixed[h * TILE : (h + 1) * TILE], joined)
            joined = joined.astype(jnp.bfloat16)
            if away:
                mixed_out[away - 1, i] = joined
            else:
                att[z, i] = joined
            return c

        lax.fori_loop(0, TILES, one, 0)
        if away:
            mixed_copy(away, True).start()

    def first_copy(away, step):
        to = lax.rem(x + step, NX)
        i = away * (NX - 1) + step - 1
        return remote(
            grad.at[away, to], first.at[away, step - 1], gs.at[i], gr.at[i], at(z, to)
        )

    def second_copy(away):
        return remote(
            partial.at[away - 1], second.at[away - 1],
            hs.at[away - 1], hr.at[away - 1], at(behind(away), x),
        )

    def gradient(away):
        if away:
            mixed_copy(away, False).wait_recv()
        grad[away] = (
            lax.dot_general(
                att[behind(away)].reshape(ROWS, GW), up_ref[...], tn,
                preferred_element_type=jnp.float32,
            )
            .astype(jnp.bfloat16)
            .reshape(NX, BLOCK, D)
        )
        for step in range(1, NX):
            first_copy(away, step).start()

    def finish_first(away):
        summed = grad[away, x].astype(jnp.float32)
        for step in range(1, NX):
            first_copy(away, step).wait_recv()
            summed += first[away, step - 1].astype(jnp.float32)
        if away:
            partial[away - 1] = summed.astype(jnp.bfloat16)
            second_copy(away).start()
        else:
            total[...] = summed

    attend(2)
    relay_out(2)
    attend(1)
    relay_out_x(1)
    attend(3)
    relay_out_x(2)
    relay_out_x(3)
    gradient(2)
    attend(0)
    gradient(1)
    gradient(0)
    finish_first(2)
    gradient(3)
    finish_first(1)

    def project_out(i, c):
        product = x_ref[i].astype(jnp.float32)
        for g in range(GROUPS):
            product += jnp.dot(
                att[g, i], owbuf[g].reshape(GW, D), preferred_element_type=jnp.float32
            )
        layer_ref[pl.ds(pl.multiple_of(i * TILE, TILE), TILE), :] = product.astype(jnp.bfloat16)
        return c

    finish_x(OUT)
    lax.fori_loop(0, TILES // 2, project_out, 0)
    finish_first(3)
    finish_first(0)
    lax.fori_loop(TILES // 2, TILES, project_out, 0)

    summed = total[...]
    for away in range(1, NZ):
        second_copy(away).wait_recv()
        summed += second[away - 1].astype(jnp.float32)
    velocity = momentum_beta * mom_ref[...] + summed
    rate = 50.0 / (500.0 + jnp.full((BLOCK, D), step_ref[0].astype(jnp.float32)))
    stepped = ow_ref[...].astype(jnp.float32) - rate * velocity
    vel_ref[...] = velocity
    pair_ref[0] = stepped.astype(jnp.bfloat16)
    pair_ref[1] = velocity.astype(jnp.bfloat16)

    for item in range(4):
        for block in range(NZ):
            for way in range(2):
                x_copy(item, block, way, True).wait_send()
                far_copy(item, block, way, True).wait_send()
    for step in range(NZ - 1):
        for up in (True, False):
            valid, _, c = out_copy(step, up, True)
            pl.when(valid)(c.wait_send)
            for t in range(TILES):
                valid, c = column_copy(t, step, up, True)
                pl.when(valid)(c.wait_send)
    for away in range(1, NZ):
        weight_copy(away, True).wait_send()
        mixed_copy(away, True).wait_send()
        second_copy(away).wait_send()
    for away in range(NZ):
        for step in range(1, NX):
            first_copy(away, step).wait_send()


def run_layer(lists, live, step, features, upstream, qkv, out, momentum):
    vmem = pl.BlockSpec(memory_space=pltpu.VMEM)
    smem = pl.BlockSpec(memory_space=pltpu.SMEM)
    bf16, f32 = jnp.bfloat16, jnp.float32

    def sems(count):
        return [pltpu.SemaphoreType.DMA((count,))] * 2

    return pl.pallas_call(
        layer_kernel,
        name="layer",
        out_shape=(
            jax.ShapeDtypeStruct((ROWS, D), bf16),
            jax.ShapeDtypeStruct((2, BLOCK, D), bf16),
            jax.ShapeDtypeStruct((BLOCK, D), f32),
        ),
        in_specs=[smem] * 3 + [vmem] * 5,
        out_specs=(vmem, vmem, vmem),
        scratch_shapes=[
            *[pltpu.VMEM((TILES, TILE, D), bf16)] * 6,
            pltpu.VMEM((GROUPS, BLOCK, 3 * GW), bf16),
            pltpu.VMEM((NZ, NX, BLOCK, 3 * GW), bf16),
            pltpu.VMEM((NZ, NX, BLOCK, D), bf16),
            pltpu.VMEM((NZ, TILES, TILE, GW), bf16),
            pltpu.VMEM((SHARDS * TILES, 2, TILE, GW), bf16),
            pltpu.VMEM((NZ - 1, TILES, TILE, GW), bf16),
            pltpu.VMEM((GROUPS, TILES, TILE, GW), bf16),
            pltpu.VMEM((GROUPS, NX, BLOCK, D), bf16),
            pltpu.VMEM((GROUPS, NX - 1, BLOCK, D), bf16),
            pltpu.VMEM((NZ - 1, BLOCK, D), bf16),
            pltpu.VMEM((NZ - 1, BLOCK, D), bf16),
            pltpu.VMEM((BLOCK, D), f32),
            *sems(6 * TILES), *sems(NZ - 1), *sems(6), *sems(8 * 4), *sems(8 * 4),
            *sems(NZ - 1), *sems(GROUPS * (NX - 1)), *sems(NZ - 1),
        ],
        compiler_params=pltpu.CompilerParams(
            collective_id=0, has_side_effects=True, vmem_limit_bytes=58 * 2**20
        ),
    )(lists, live, step, features, upstream, qkv, out, momentum)


def swap(bit, pair):
    def with_bit(number):
        return lambda p: lax.ppermute(
            p, "rep", [(i, i ^ 1 << number) for i in range(lax.axis_size("rep"))]
        )

    count = lax.axis_size("rep").bit_length() - 1
    return lax.switch(bit % count, [with_bit(n) for n in range(count)], pair)


def body(
    cell_features, upstream, qkv_weight, out_weight, momentum, key_tiles, live_blocks, step_index
):
    layer_out, pair, velocity = run_layer(
        key_tiles[0], live_blocks[0], step_index.reshape(1),
        cell_features[0].reshape(TILES, TILE, D), upstream[0],
        qkv_weight[0], out_weight[0], momentum[0],
    )
    other = swap(step_index, pair)
    stepped = pair[0].astype(jnp.float32) + other[0].astype(jnp.float32)
    new_weight = (0.5 * stepped).astype(jnp.bfloat16)
    new_momentum = 0.5 * (velocity + other[1].astype(jnp.float32))
    return layer_out[None], new_weight[None], new_momentum[None]


def solution(mesh):
    rows = P("rep", "shard", None)
    placed = (rows, rows, rows, rows, rows, P("rep", None, None), P("rep", None), P())
    return jax.shard_map(
        body, mesh=mesh, in_specs=placed, out_specs=(rows, rows, rows), check_vma=False
    )
```

```python
import functools

import jax
import jax.numpy as jnp
from jax import lax
from jax.experimental import pallas as pl
from jax.experimental.pallas import tpu as pltpu
from jax.sharding import PartitionSpec as P

HEADS = 16
HEAD_DIM = 64
TILE = 128
KB = 6
TILES = 4
NX = 4
NZ = 4
SHARDS = NX * NZ
PARTNERS = 4
GROUPS = NZ
D = 1024
GW = D // GROUPS
BLOCK = D // SHARDS
ROWS = TILES * TILE
MESH = pl.DeviceIdType.MESH

momentum_beta = 0.9


def at(z, x):
    return {"shard": z * NX + x}


def remote(src, dst, send, recv, device):
    return pltpu.make_async_remote_copy(
        src_ref=src, dst_ref=dst, send_sem=send, recv_sem=recv, device_id=device, device_id_type=MESH
    )


def layer_kernel(
    lists_ref, live_ref, step_ref, x_ref, up_ref, w_ref, ow_ref, mom_ref,
    layer_ref, sent_ref, theirs_ref, vel_ref,
    below0, below1, below2, above0, above1, above2,
    wparts, wbuf, owbuf, qbuf, kvbuf, mixed_out, att, grad, first, partial, second, total, theirs,
    ps, pr, cs, cr, ws, wr, zs, zr, ds, dr, es, er, as_, ar, gs, gr, hs, hr,
):
    me = lax.axis_index("shard")
    z, x = lax.div(me, NX), lax.rem(me, NX)
    right, left, far = (lax.rem(x + k, NX) for k in (1, NX - 1, NX // 2))
    ways = ((0, right, left), (1, left, right))

    def behind(away):
        return lax.rem(z - away + NZ, NZ)

    def ahead(away):
        return lax.rem(z + away, NZ)

    barrier = pltpu.get_barrier_semaphore()
    peers = [at(z, lax.rem(x + k, NX)) for k in range(1, NX)]
    peers += [at(lax.rem(z + k, NZ), x) for k in range(1, NZ)]
    rep = lax.axis_index("rep")
    partners = [
        rep + (1 << bit) * (1 - 2 * lax.rem(lax.div(rep, 1 << bit), 2)) for bit in range(PARTNERS)
    ]
    peers += [{"rep": other} for other in partners]
    for peer in peers:
        pl.semaphore_signal(barrier, 1, device_id=peer, device_id_type=MESH)
    for g in range(GROUPS):
        for part in range(3):
            wparts[g, :, pl.ds(part * GW, GW)] = w_ref[:, pl.ds(part * D + g * GW, GW)]
    wbuf[z, x] = wparts[z]
    owbuf[z, x] = ow_ref[...]
    pl.semaphore_wait(barrier, len(peers))

    def along_z(step, up, sending):
        came = z if sending else (z - 1 if up else z + 1)
        block = came - step if up else came + step
        valid = (block >= 0) & (block < NZ)
        if sending:
            valid &= (z < NZ - 1) if up else (z > 0)
        return valid, lax.rem(block + 2 * NZ, NZ), at(lax.rem(z + (1 if up else NZ - 1), NZ), x)

    W, OUT, PAIRS = 0, 1, (2, 3)

    def view(item, block, column, half=None):
        if item in PAIRS:
            base = (block * NX + column) * TILES + (item - PAIRS[0]) * 2
            return kvbuf.at[pl.ds(base, 2)] if half is None else kvbuf.at[pl.ds(base + half, 1)]
        ref = (wbuf if item == W else owbuf).at[block, column]
        return ref if half is None else ref.at[pl.ds(half * (BLOCK // 2), BLOCK // 2)]

    def x_copy(item, block, way, sending):
        _, to, back = ways[way]
        j = item * 8 + block * 2 + way
        ref = view(item, block, x if sending else back)
        return remote(ref, ref, ds.at[j], dr.at[j], at(z, to))

    def far_copy(item, block, way, sending):
        _, to, back = ways[way]
        j = item * 8 + block * 2 + way
        ref = view(item, block, back if sending else far, way)
        return remote(ref, ref, es.at[j], er.at[j], at(z, to))

    def share_x(item, block):
        for way in range(2):
            x_copy(item, block, way, True).start()

    def relay_x(item, block):
        for way in range(2):
            x_copy(item, block, way, False).wait_recv()
            far_copy(item, block, way, True).start()

    def finish_x(item):
        for block in range(NZ):
            for way in range(2):
                far_copy(item, block, way, False).wait_recv()

    def at_offset(offset, act):
        block = z + offset

        @pl.when((block >= 0) & (block < NZ))
        def _():
            act(lax.rem(block + NZ, NZ))

    def weight_copy(away, sending):
        to = ahead(away)
        return remote(
            wparts.at[to], wbuf.at[z if sending else behind(away), x],
            ws.at[away - 1], wr.at[away - 1], at(to, x),
        )

    blocks = {0: x_ref, -1: below0, -2: below1, -3: below2, 1: above0, 2: above1, 3: above2}

    def column_copy(t, step, up, sending):
        valid, _, to = along_z(step, up, sending)
        sign = -1 if up else 1
        j = (step * 2 + (0 if up else 1)) * TILES + t
        return valid, remote(
            blocks[sign * step].at[t], blocks[sign * (step + 1)].at[t], cs.at[j], cr.at[j], to
        )

    def start_column(t):
        for up in (True, False):
            valid, c = column_copy(t, 0, up, True)
            pl.when(valid)(c.start)

    def relay_column(t, step):
        for up in (True, False):
            valid, c = column_copy(t, step, up, False)

            @pl.when(valid)
            def _():
                c.wait_recv()
                if step + 1 < NZ - 1:
                    more, onward = column_copy(t, step + 1, up, True)
                    pl.when(more)(onward.start)

    def partner_copy(bit):
        return remote(ow_ref, theirs.at[bit], ps.at[bit], pr.at[bit], {"rep": partners[bit]})

    def out_copy(step, up, sending):
        valid, block, to = along_z(step, up, sending)
        j = step * 2 + (0 if up else 1)
        ref = owbuf.at[block, x]
        return valid, block, remote(ref, ref, zs.at[j], zr.at[j], to)

    def start_out():
        for up in (True, False):
            valid, _, c = out_copy(0, up, True)
            pl.when(valid)(c.start)

    def relay_out(step):
        for up in (True, False):
            valid, block, c = out_copy(step, up, False)

            @pl.when(valid)
            def _():
                c.wait_recv()
                if step + 1 < NZ - 1:
                    more, _, onward = out_copy(step + 1, up, True)
                    pl.when(more)(onward.start)
                share_x(OUT, block)

    def project(pair, block, rows):
        whole = jnp.dot(
            rows[pl.ds(pair * 2, 2)].reshape(2 * TILE, D), wbuf[...].reshape(D, 3 * GW),
            preferred_element_type=jnp.float32,
        ).astype(jnp.bfloat16).reshape(2, TILE, 3 * GW)
        base = pl.ds((block * NX + x) * TILES + pair * 2, 2)
        kvbuf[base, 0] = whole[:, :, GW : 2 * GW]
        kvbuf[base, 1] = whole[:, :, 2 * GW :]
        share_x(PAIRS[pair], block)
        qbuf[block, pl.ds(pair * 2, 2)] = whole[:, :, 0:GW] * jnp.bfloat16(HEAD_DIM ** -0.5)

    def both(distance, act):
        for offset in (-distance, distance):
            at_offset(offset, functools.partial(act, offset))

    def project_at(distance, pair):
        both(distance, lambda offset, block: project(pair, block, blocks[offset]))

    def relay_keys(distance, pair):
        both(distance, lambda offset, block: relay_x(PAIRS[pair], block))

    def relay_out_x(distance):
        both(distance, lambda offset, block: relay_x(OUT, block))

    for away in (1, 3, 2):
        weight_copy(away, True).start()
    share_x(W, z)
    share_x(OUT, z)
    for away in (1, 3):
        weight_copy(away, False).wait_recv()
        share_x(W, behind(away))
    start_column(0)
    weight_copy(2, False).wait_recv()
    share_x(W, behind(2))
    start_column(1)
    for away in (0, 1, 3, 2):
        relay_x(W, behind(away))
    start_column(2)
    finish_x(W)
    start_column(3)

    project(0, z, x_ref)
    relay_column(0, 0)
    project(1, z, x_ref)
    relay_x(PAIRS[0], z)
    relay_column(1, 0)
    project_at(1, 0)
    relay_x(PAIRS[1], z)
    relay_column(2, 0)
    relay_column(3, 0)
    project_at(1, 1)
    relay_column(0, 1)
    relay_keys(1, 0)
    relay_column(1, 1)
    project_at(2, 0)
    relay_keys(1, 1)
    relay_column(2, 1)
    relay_column(3, 1)
    project_at(2, 1)
    relay_keys(2, 0)
    relay_column(0, 2)
    relay_column(1, 2)
    start_out()
    for bit in range(PARTNERS):
        partner_copy(bit).start()
    project_at(3, 0)
    relay_keys(2, 1)
    relay_column(2, 2)
    relay_column(3, 2)
    project_at(3, 1)
    relay_out(0)
    relay_x(OUT, z)
    relay_keys(3, 0)
    relay_keys(3, 1)
    relay_out(1)
    for pair in PAIRS:
        finish_x(pair)

    lane_head = lax.broadcasted_iota(jnp.int32, (TILE, GW), 1) // HEAD_DIM
    slot_of = lax.broadcasted_iota(jnp.int32, (1, KB * TILE), 1) // TILE
    nt = (((1,), (1,)), ((), ()))
    tn = (((0,), (0,)), ((), ()))

    def mixed_copy(away, sending):
        return remote(
            mixed_out.at[away - 1], att.at[z if sending else behind(away)],
            as_.at[away - 1], ar.at[away - 1], at(ahead(away), x),
        )

    def attend(away):
        block = ahead(away)

        def one(i, c):
            tile = (block * NX + x) * TILES + i
            live = live_ref[tile]
            keys, values = [], []
            for j in range(KB):
                listed = lists_ref[tile, j]
                keys.append(kvbuf[listed, 0])
                values.append(kvbuf[listed, 1])
            q = qbuf[block, i]
            masked = jnp.concatenate(
                [jnp.where(lane_head == h, q, jnp.bfloat16(0)) for h in range(GW // HEAD_DIM)], axis=0
            )
            scores = lax.dot_general(
                masked, jnp.concatenate(keys, axis=0), nt, preferred_element_type=jnp.float32
            )
            scores = jnp.where(slot_of < live, scores, jnp.float32(-1e30))
            exponent = jnp.exp(scores - jnp.max(scores, axis=1, keepdims=True))
            scale = 1.0 / jnp.sum(exponent, axis=1, keepdims=True)
            mixed = jnp.dot(
                exponent.astype(jnp.bfloat16), jnp.concatenate(values, axis=0),
                preferred_element_type=jnp.float32,
            ) * scale
            joined = jnp.zeros((TILE, GW), jnp.float32)
            for h in range(GW // HEAD_DIM):
                joined = jnp.where(lane_head == h, mixed[h * TILE : (h + 1) * TILE], joined)
            joined = joined.astype(jnp.bfloat16)
            if away:
                mixed_out[away - 1, i] = joined
            else:
                att[z, i] = joined
            return c

        lax.fori_loop(0, TILES, one, 0, unroll=TILES)
        if away:
            mixed_copy(away, True).start()

    def first_copy(away, step):
        to = lax.rem(x + step, NX)
        i = away * (NX - 1) + step - 1
        return remote(
            grad.at[away, to], first.at[away, step - 1], gs.at[i], gr.at[i], at(z, to)
        )

    def second_copy(away):
        return remote(
            partial.at[away - 1], second.at[away - 1],
            hs.at[away - 1], hr.at[away - 1], at(behind(away), x),
        )

    def gradient(away):
        if away:
            mixed_copy(away, False).wait_recv()
        grad[away] = (
            lax.dot_general(
                att[behind(away)].reshape(ROWS, GW), up_ref[...], tn,
                preferred_element_type=jnp.float32,
            )
            .astype(jnp.bfloat16)
            .reshape(NX, BLOCK, D)
        )
        for step in range(1, NX):
            first_copy(away, step).start()

    def finish_first(away):
        summed = grad[away, x].astype(jnp.float32)
        for step in range(1, NX):
            first_copy(away, step).wait_recv()
            summed += first[away, step - 1].astype(jnp.float32)
        if away:
            partial[away - 1] = summed.astype(jnp.bfloat16)
            second_copy(away).start()
        else:
            total[...] = summed

    attend(2)
    relay_out(2)
    attend(1)
    relay_out_x(1)
    attend(3)
    attend(0)
    gradient(0)
    relay_out_x(2)
    relay_out_x(3)
    gradient(2)
    finish_first(0)
    gradient(1)
    finish_first(2)
    gradient(3)
    finish_first(1)

    def project_out(i, c):
        product = x_ref[i].astype(jnp.float32)
        for g in range(GROUPS):
            product += jnp.dot(
                att[g, i], owbuf[g].reshape(GW, D), preferred_element_type=jnp.float32
            )
        layer_ref[pl.ds(pl.multiple_of(i * TILE, TILE), TILE), :] = product.astype(jnp.bfloat16)
        return c

    finish_x(OUT)
    lax.fori_loop(0, TILES // 2, project_out, 0)
    finish_first(3)
    lax.fori_loop(TILES // 2, TILES, project_out, 0)

    summed = total[...]
    for away in range(1, NZ):
        second_copy(away).wait_recv()
        summed += second[away - 1].astype(jnp.float32)
    velocity = momentum_beta * mom_ref[...] + summed
    vel_ref[...] = velocity
    sent_ref[...] = velocity.astype(jnp.bfloat16)
    for bit in range(PARTNERS):
        partner_copy(bit).wait_recv()
    theirs_ref[...] = theirs[lax.rem(step_ref[0], PARTNERS)]

    for item in range(4):
        for block in range(NZ):
            for way in range(2):
                x_copy(item, block, way, True).wait_send()
                far_copy(item, block, way, True).wait_send()
    for step in range(NZ - 1):
        for up in (True, False):
            valid, _, c = out_copy(step, up, True)
            pl.when(valid)(c.wait_send)
            for t in range(TILES):
                valid, c = column_copy(t, step, up, True)
                pl.when(valid)(c.wait_send)
    for away in range(1, NZ):
        weight_copy(away, True).wait_send()
        mixed_copy(away, True).wait_send()
        second_copy(away).wait_send()
    for away in range(NZ):
        for step in range(1, NX):
            first_copy(away, step).wait_send()
    for bit in range(PARTNERS):
        partner_copy(bit).wait_send()


def run_layer(lists, live, step, features, upstream, qkv, out, momentum):
    vmem = pl.BlockSpec(memory_space=pltpu.VMEM)
    smem = pl.BlockSpec(memory_space=pltpu.SMEM)
    bf16, f32 = jnp.bfloat16, jnp.float32

    def sems(count):
        return [pltpu.SemaphoreType.DMA((count,))] * 2

    return pl.pallas_call(
        layer_kernel,
        name="layer",
        out_shape=(
            jax.ShapeDtypeStruct((ROWS, D), bf16),
            jax.ShapeDtypeStruct((BLOCK, D), bf16),
            jax.ShapeDtypeStruct((BLOCK, D), bf16),
            jax.ShapeDtypeStruct((BLOCK, D), f32),
        ),
        in_specs=[smem] * 3 + [vmem] * 5,
        out_specs=(vmem,) * 4,
        scratch_shapes=[
            *[pltpu.VMEM((TILES, TILE, D), bf16)] * 6,
            pltpu.VMEM((GROUPS, BLOCK, 3 * GW), bf16),
            pltpu.VMEM((NZ, NX, BLOCK, 3 * GW), bf16),
            pltpu.VMEM((NZ, NX, BLOCK, D), bf16),
            pltpu.VMEM((NZ, TILES, TILE, GW), bf16),
            pltpu.VMEM((SHARDS * TILES, 2, TILE, GW), bf16),
            pltpu.VMEM((NZ - 1, TILES, TILE, GW), bf16),
            pltpu.VMEM((GROUPS, TILES, TILE, GW), bf16),
            pltpu.VMEM((GROUPS, NX, BLOCK, D), bf16),
            pltpu.VMEM((GROUPS, NX - 1, BLOCK, D), bf16),
            pltpu.VMEM((NZ - 1, BLOCK, D), bf16),
            pltpu.VMEM((NZ - 1, BLOCK, D), bf16),
            pltpu.VMEM((BLOCK, D), f32),
            pltpu.VMEM((PARTNERS, BLOCK, D), bf16),
            *sems(PARTNERS), *sems(6 * TILES), *sems(NZ - 1), *sems(6), *sems(8 * 4), *sems(8 * 4),
            *sems(NZ - 1), *sems(GROUPS * (NX - 1)), *sems(NZ - 1),
        ],
        compiler_params=pltpu.CompilerParams(
            collective_id=0, has_side_effects=True, vmem_limit_bytes=58 * 2**20
        ),
    )(lists, live, step, features, upstream, qkv, out, momentum)


def average_kernel(step_ref, vel_ref, other_vel_ref, ow_ref, other_ow_ref, weight_ref, momentum_ref):
    rate = 50.0 / (500.0 + jnp.full((BLOCK, D), step_ref[0].astype(jnp.float32)))
    velocity, other = vel_ref[...], other_vel_ref[...].astype(jnp.float32)

    def stepped(weight, moved):
        moved = weight.astype(jnp.float32) - rate * moved
        return moved.astype(jnp.bfloat16).astype(jnp.float32)

    both = stepped(ow_ref[...], velocity) + stepped(other_ow_ref[...], other)
    weight_ref[...] = (0.5 * both).astype(jnp.bfloat16)
    momentum_ref[...] = 0.5 * (velocity + other)


def average(step, velocity, other_velocity, out, other_out):
    vmem = pl.BlockSpec(memory_space=pltpu.VMEM)
    return pl.pallas_call(
        average_kernel,
        name="average",
        out_shape=(
            jax.ShapeDtypeStruct((BLOCK, D), jnp.bfloat16),
            jax.ShapeDtypeStruct((BLOCK, D), jnp.float32),
        ),
        in_specs=[pl.BlockSpec(memory_space=pltpu.SMEM)] + [vmem] * 4,
        out_specs=(vmem, vmem),
    )(step, velocity, other_velocity, out, other_out)


def swap(bit, sent):
    def with_bit(number):
        return lambda value: lax.ppermute(
            value, "rep", [(i, i ^ 1 << number) for i in range(1 << PARTNERS)]
        )

    return lax.switch(bit % PARTNERS, [with_bit(n) for n in range(PARTNERS)], sent)


def body(
    cell_features, upstream, qkv_weight, out_weight, momentum, key_tiles, live_blocks, step_index
):
    step = step_index.reshape(1)
    layer_out, sent, theirs, velocity = run_layer(
        key_tiles[0], live_blocks[0], step,
        cell_features[0].reshape(TILES, TILE, D), upstream[0],
        qkv_weight[0], out_weight[0], momentum[0],
    )
    other = swap(step_index, sent)
    new_weight, new_momentum = average(step, velocity, other, out_weight[0], theirs)
    return layer_out[None], new_weight[None], new_momentum[None]


def solution(mesh):
    rows = P("rep", "shard", None)
    placed = (rows, rows, rows, rows, rows, P("rep", None, None), P("rep", None), P())
    return jax.shard_map(
        body, mesh=mesh, in_specs=placed, out_specs=(rows, rows, rows), check_vma=False
    )
```

```python
import functools

import jax
import jax.numpy as jnp
from jax import lax
from jax.experimental import pallas as pl
from jax.experimental.pallas import tpu as pltpu
from jax.sharding import PartitionSpec as P

HEADS = 16
HEAD_DIM = 64
TILE = 128
KB = 6
TILES = 4
NX = 4
NZ = 4
SHARDS = NX * NZ
PARTNERS = 4
GROUPS = NZ
D = 1024
GW = D // GROUPS
BLOCK = D // SHARDS
ROWS = TILES * TILE
MESH = pl.DeviceIdType.MESH

momentum_beta = 0.9


def at(z, x):
    return {"shard": z * NX + x}


def remote(src, dst, send, recv, device):
    return pltpu.make_async_remote_copy(
        src_ref=src, dst_ref=dst, send_sem=send, recv_sem=recv, device_id=device, device_id_type=MESH
    )


def layer_kernel(
    lists_ref, live_ref, step_ref, x_ref, up_ref, w_ref, ow_ref, mom_ref,
    layer_ref, sent_ref, theirs_ref, vel_ref,
    below0, below1, below2, above0, above1, above2,
    wparts, wbuf, owbuf, qbuf, kvbuf, mixed_out, att, grad, first, partial, second, total, theirs,
    ps, pr, cs, cr, ws, wr, zs, zr, ds, dr, es, er, as_, ar, gs, gr, hs, hr,
):
    me = lax.axis_index("shard")
    z, x = lax.div(me, NX), lax.rem(me, NX)
    right, left, far = (lax.rem(x + k, NX) for k in (1, NX - 1, NX // 2))
    ways = ((0, right, left), (1, left, right))

    def behind(away):
        return lax.rem(z - away + NZ, NZ)

    def ahead(away):
        return lax.rem(z + away, NZ)

    barrier = pltpu.get_barrier_semaphore()
    peers = [at(z, lax.rem(x + k, NX)) for k in range(1, NX)]
    peers += [at(lax.rem(z + k, NZ), x) for k in range(1, NZ)]
    rep = lax.axis_index("rep")
    partners = [
        rep + (1 << bit) * (1 - 2 * lax.rem(lax.div(rep, 1 << bit), 2)) for bit in range(PARTNERS)
    ]
    peers += [{"rep": other} for other in partners]
    for peer in peers:
        pl.semaphore_signal(barrier, 1, device_id=peer, device_id_type=MESH)
    for g in range(GROUPS):
        for part in range(3):
            wparts[g, :, pl.ds(part * GW, GW)] = w_ref[:, pl.ds(part * D + g * GW, GW)]
    wbuf[z, x] = wparts[z]
    owbuf[z, x] = ow_ref[...]
    pl.semaphore_wait(barrier, len(peers))

    def along_z(step, up, sending):
        came = z if sending else (z - 1 if up else z + 1)
        block = came - step if up else came + step
        valid = (block >= 0) & (block < NZ)
        if sending:
            valid &= (z < NZ - 1) if up else (z > 0)
        return valid, lax.rem(block + 2 * NZ, NZ), at(lax.rem(z + (1 if up else NZ - 1), NZ), x)

    W, OUT, PAIRS = 0, 1, (2, 3)

    def view(item, block, column, half=None):
        if item in PAIRS:
            base = (block * NX + column) * TILES + (item - PAIRS[0]) * 2
            return kvbuf.at[pl.ds(base, 2)] if half is None else kvbuf.at[pl.ds(base + half, 1)]
        ref = (wbuf if item == W else owbuf).at[block, column]
        return ref if half is None else ref.at[pl.ds(half * (BLOCK // 2), BLOCK // 2)]

    def x_copy(item, block, way, sending):
        _, to, back = ways[way]
        j = item * 8 + block * 2 + way
        ref = view(item, block, x if sending else back)
        return remote(ref, ref, ds.at[j], dr.at[j], at(z, to))

    def far_copy(item, block, way, sending):
        _, to, back = ways[way]
        j = item * 8 + block * 2 + way
        ref = view(item, block, back if sending else far, way)
        return remote(ref, ref, es.at[j], er.at[j], at(z, to))

    def share_x(item, block):
        for way in range(2):
            x_copy(item, block, way, True).start()

    def relay_x(item, block):
        for way in range(2):
            x_copy(item, block, way, False).wait_recv()
            far_copy(item, block, way, True).start()

    def finish_x(item):
        for block in range(NZ):
            for way in range(2):
                far_copy(item, block, way, False).wait_recv()

    def at_offset(offset, act):
        block = z + offset

        @pl.when((block >= 0) & (block < NZ))
        def _():
            act(lax.rem(block + NZ, NZ))

    def weight_copy(away, sending):
        to = ahead(away)
        return remote(
            wparts.at[to], wbuf.at[z if sending else behind(away), x],
            ws.at[away - 1], wr.at[away - 1], at(to, x),
        )

    blocks = {0: x_ref, -1: below0, -2: below1, -3: below2, 1: above0, 2: above1, 3: above2}

    def column_copy(t, step, up, sending):
        valid, _, to = along_z(step, up, sending)
        sign = -1 if up else 1
        j = (step * 2 + (0 if up else 1)) * TILES + t
        return valid, remote(
            blocks[sign * step].at[t], blocks[sign * (step + 1)].at[t], cs.at[j], cr.at[j], to
        )

    def start_column(t):
        for up in (True, False):
            valid, c = column_copy(t, 0, up, True)
            pl.when(valid)(c.start)

    def relay_column(t, step):
        for up in (True, False):
            valid, c = column_copy(t, step, up, False)

            @pl.when(valid)
            def _():
                c.wait_recv()
                if step + 1 < NZ - 1:
                    more, onward = column_copy(t, step + 1, up, True)
                    pl.when(more)(onward.start)

    def partner_copy(bit):
        return remote(ow_ref, theirs.at[bit], ps.at[bit], pr.at[bit], {"rep": partners[bit]})

    def out_copy(step, up, sending):
        valid, block, to = along_z(step, up, sending)
        j = step * 2 + (0 if up else 1)
        ref = owbuf.at[block]
        return valid, remote(ref, ref, zs.at[j], zr.at[j], to)

    def start_out():
        for up in (True, False):
            valid, c = out_copy(0, up, True)
            pl.when(valid)(c.start)

    def relay_out(step):
        for up in (True, False):
            valid, c = out_copy(step, up, False)

            @pl.when(valid)
            def _():
                c.wait_recv()
                if step + 1 < NZ - 1:
                    more, onward = out_copy(step + 1, up, True)
                    pl.when(more)(onward.start)

    def project(pair, block, rows):
        whole = jnp.dot(
            rows[pl.ds(pair * 2, 2)].reshape(2 * TILE, D), wbuf[...].reshape(D, 3 * GW),
            preferred_element_type=jnp.float32,
        ).astype(jnp.bfloat16).reshape(2, TILE, 3 * GW)
        base = pl.ds((block * NX + x) * TILES + pair * 2, 2)
        kvbuf[base, 0] = whole[:, :, GW : 2 * GW]
        kvbuf[base, 1] = whole[:, :, 2 * GW :]
        share_x(PAIRS[pair], block)
        qbuf[block, pl.ds(pair * 2, 2)] = whole[:, :, 0:GW] * jnp.bfloat16(HEAD_DIM ** -0.5)

    def both(distance, act):
        for offset in (-distance, distance):
            at_offset(offset, functools.partial(act, offset))

    def project_at(distance, pair):
        both(distance, lambda offset, block: project(pair, block, blocks[offset]))

    def relay_keys(distance, pair):
        both(distance, lambda offset, block: relay_x(PAIRS[pair], block))

    for away in (1, 3, 2):
        weight_copy(away, True).start()
    share_x(W, z)
    share_x(OUT, z)
    for away in (1, 3):
        weight_copy(away, False).wait_recv()
        share_x(W, behind(away))
    start_column(0)
    weight_copy(2, False).wait_recv()
    share_x(W, behind(2))
    start_column(1)
    for away in (0, 1, 3, 2):
        relay_x(W, behind(away))
    relay_x(OUT, z)
    start_column(2)
    finish_x(W)
    start_column(3)

    project(0, z, x_ref)
    relay_column(0, 0)
    project(1, z, x_ref)
    relay_x(PAIRS[0], z)
    relay_column(1, 0)
    project_at(1, 0)
    relay_x(PAIRS[1], z)
    relay_column(2, 0)
    relay_column(3, 0)
    project_at(1, 1)
    relay_column(0, 1)
    relay_keys(1, 0)
    relay_column(1, 1)
    project_at(2, 0)
    relay_keys(1, 1)
    relay_column(2, 1)
    relay_column(3, 1)
    project_at(2, 1)
    relay_keys(2, 0)
    relay_column(0, 2)
    relay_column(1, 2)
    for way in range(2):
        far_copy(OUT, z, way, False).wait_recv()
    start_out()
    for bit in range(PARTNERS):
        partner_copy(bit).start()
    project_at(3, 0)
    relay_keys(2, 1)
    relay_column(2, 2)
    relay_column(3, 2)
    project_at(3, 1)
    relay_keys(3, 0)
    relay_out(0)
    relay_keys(3, 1)
    for pair in PAIRS:
        finish_x(pair)

    lane_head = lax.broadcasted_iota(jnp.int32, (TILE, GW), 1) // HEAD_DIM
    slot_of = lax.broadcasted_iota(jnp.int32, (1, KB * TILE), 1) // TILE
    nt = (((1,), (1,)), ((), ()))
    tn = (((0,), (0,)), ((), ()))

    def mixed_copy(away, sending):
        return remote(
            mixed_out.at[away - 1], att.at[z if sending else behind(away)],
            as_.at[away - 1], ar.at[away - 1], at(ahead(away), x),
        )

    def attend(away):
        block = ahead(away)

        def one(i, c):
            tile = (block * NX + x) * TILES + i
            live = live_ref[tile]
            keys, values = [], []
            for j in range(KB):
                listed = lists_ref[tile, j]
                keys.append(kvbuf[listed, 0])
                values.append(kvbuf[listed, 1])
            q = qbuf[block, i]
            masked = jnp.concatenate(
                [jnp.where(lane_head == h, q, jnp.bfloat16(0)) for h in range(GW // HEAD_DIM)], axis=0
            )
            scores = lax.dot_general(
                masked, jnp.concatenate(keys, axis=0), nt, preferred_element_type=jnp.float32
            )
            scores = jnp.where(slot_of < live, scores, jnp.float32(-1e30))
            exponent = jnp.exp(scores - jnp.max(scores, axis=1, keepdims=True))
            scale = 1.0 / jnp.sum(exponent, axis=1, keepdims=True)
            mixed = jnp.dot(
                exponent.astype(jnp.bfloat16), jnp.concatenate(values, axis=0),
                preferred_element_type=jnp.float32,
            ) * scale
            joined = jnp.zeros((TILE, GW), jnp.float32)
            for h in range(GW // HEAD_DIM):
                joined = jnp.where(lane_head == h, mixed[h * TILE : (h + 1) * TILE], joined)
            joined = joined.astype(jnp.bfloat16)
            if away:
                mixed_out[away - 1, i] = joined
            else:
                att[z, i] = joined
            return c

        lax.fori_loop(0, TILES, one, 0, unroll=TILES)
        if away:
            mixed_copy(away, True).start()

    def first_copy(away, step):
        to = lax.rem(x + step, NX)
        i = away * (NX - 1) + step - 1
        return remote(
            grad.at[away, to], first.at[away, step - 1], gs.at[i], gr.at[i], at(z, to)
        )

    def second_copy(away):
        return remote(
            partial.at[away - 1], second.at[away - 1],
            hs.at[away - 1], hr.at[away - 1], at(behind(away), x),
        )

    def gradient(away):
        if away:
            mixed_copy(away, False).wait_recv()
        grad[away] = (
            lax.dot_general(
                att[behind(away)].reshape(ROWS, GW), up_ref[...], tn,
                preferred_element_type=jnp.float32,
            )
            .astype(jnp.bfloat16)
            .reshape(NX, BLOCK, D)
        )
        for step in range(1, NX):
            first_copy(away, step).start()

    def finish_first(away):
        summed = grad[away, x].astype(jnp.float32)
        for step in range(1, NX):
            first_copy(away, step).wait_recv()
            summed += first[away, step - 1].astype(jnp.float32)
        if away:
            partial[away - 1] = summed.astype(jnp.bfloat16)
            second_copy(away).start()
        else:
            total[...] = summed

    attend(2)
    relay_out(1)
    attend(1)
    attend(3)
    attend(0)
    gradient(0)
    gradient(2)
    finish_first(0)
    gradient(1)
    finish_first(2)
    gradient(3)
    finish_first(1)

    def project_out(i, c):
        product = x_ref[i].astype(jnp.float32)
        for g in range(GROUPS):
            product += jnp.dot(
                att[g, i], owbuf[g].reshape(GW, D), preferred_element_type=jnp.float32
            )
        layer_ref[pl.ds(pl.multiple_of(i * TILE, TILE), TILE), :] = product.astype(jnp.bfloat16)
        return c

    relay_out(2)
    lax.fori_loop(0, TILES // 2, project_out, 0)
    finish_first(3)
    lax.fori_loop(TILES // 2, TILES, project_out, 0)

    summed = total[...]
    for away in range(1, NZ):
        second_copy(away).wait_recv()
        summed += second[away - 1].astype(jnp.float32)
    velocity = momentum_beta * mom_ref[...] + summed
    vel_ref[...] = velocity
    sent_ref[...] = velocity.astype(jnp.bfloat16)
    for bit in range(PARTNERS):
        partner_copy(bit).wait_recv()
    theirs_ref[...] = theirs[lax.rem(step_ref[0], PARTNERS)]

    for way in range(2):
        x_copy(OUT, z, way, True).wait_send()
        far_copy(OUT, z, way, True).wait_send()
        for item in (W, *PAIRS):
            for block in range(NZ):
                x_copy(item, block, way, True).wait_send()
                far_copy(item, block, way, True).wait_send()
    for step in range(NZ - 1):
        for up in (True, False):
            valid, c = out_copy(step, up, True)
            pl.when(valid)(c.wait_send)
            for t in range(TILES):
                valid, c = column_copy(t, step, up, True)
                pl.when(valid)(c.wait_send)
    for away in range(1, NZ):
        weight_copy(away, True).wait_send()
        mixed_copy(away, True).wait_send()
        second_copy(away).wait_send()
    for away in range(NZ):
        for step in range(1, NX):
            first_copy(away, step).wait_send()
    for bit in range(PARTNERS):
        partner_copy(bit).wait_send()


def run_layer(lists, live, step, features, upstream, qkv, out, momentum):
    vmem = pl.BlockSpec(memory_space=pltpu.VMEM)
    smem = pl.BlockSpec(memory_space=pltpu.SMEM)
    bf16, f32 = jnp.bfloat16, jnp.float32

    def sems(count):
        return [pltpu.SemaphoreType.DMA((count,))] * 2

    return pl.pallas_call(
        layer_kernel,
        name="layer",
        out_shape=(
            jax.ShapeDtypeStruct((ROWS, D), bf16),
            jax.ShapeDtypeStruct((BLOCK, D), bf16),
            jax.ShapeDtypeStruct((BLOCK, D), bf16),
            jax.ShapeDtypeStruct((BLOCK, D), f32),
        ),
        in_specs=[smem] * 3 + [vmem] * 5,
        out_specs=(vmem,) * 4,
        scratch_shapes=[
            *[pltpu.VMEM((TILES, TILE, D), bf16)] * 6,
            pltpu.VMEM((GROUPS, BLOCK, 3 * GW), bf16),
            pltpu.VMEM((NZ, NX, BLOCK, 3 * GW), bf16),
            pltpu.VMEM((NZ, NX, BLOCK, D), bf16),
            pltpu.VMEM((NZ, TILES, TILE, GW), bf16),
            pltpu.VMEM((SHARDS * TILES, 2, TILE, GW), bf16),
            pltpu.VMEM((NZ - 1, TILES, TILE, GW), bf16),
            pltpu.VMEM((GROUPS, TILES, TILE, GW), bf16),
            pltpu.VMEM((GROUPS, NX, BLOCK, D), bf16),
            pltpu.VMEM((GROUPS, NX - 1, BLOCK, D), bf16),
            pltpu.VMEM((NZ - 1, BLOCK, D), bf16),
            pltpu.VMEM((NZ - 1, BLOCK, D), bf16),
            pltpu.VMEM((BLOCK, D), f32),
            pltpu.VMEM((PARTNERS, BLOCK, D), bf16),
            *sems(PARTNERS), *sems(6 * TILES), *sems(NZ - 1), *sems(6), *sems(8 * 4), *sems(8 * 4),
            *sems(NZ - 1), *sems(GROUPS * (NX - 1)), *sems(NZ - 1),
        ],
        compiler_params=pltpu.CompilerParams(
            collective_id=0, has_side_effects=True, vmem_limit_bytes=58 * 2**20
        ),
    )(lists, live, step, features, upstream, qkv, out, momentum)


def average_kernel(step_ref, vel_ref, other_vel_ref, ow_ref, other_ow_ref, weight_ref, momentum_ref):
    rate = 50.0 / (500.0 + jnp.full((BLOCK, D), step_ref[0].astype(jnp.float32)))
    velocity, other = vel_ref[...], other_vel_ref[...].astype(jnp.float32)

    def stepped(weight, moved):
        moved = weight.astype(jnp.float32) - rate * moved
        return moved.astype(jnp.bfloat16).astype(jnp.float32)

    both = stepped(ow_ref[...], velocity) + stepped(other_ow_ref[...], other)
    weight_ref[...] = (0.5 * both).astype(jnp.bfloat16)
    momentum_ref[...] = 0.5 * (velocity + other)


def average(step, velocity, other_velocity, out, other_out):
    vmem = pl.BlockSpec(memory_space=pltpu.VMEM)
    return pl.pallas_call(
        average_kernel,
        name="average",
        out_shape=(
            jax.ShapeDtypeStruct((BLOCK, D), jnp.bfloat16),
            jax.ShapeDtypeStruct((BLOCK, D), jnp.float32),
        ),
        in_specs=[pl.BlockSpec(memory_space=pltpu.SMEM)] + [vmem] * 4,
        out_specs=(vmem, vmem),
    )(step, velocity, other_velocity, out, other_out)


def swap(bit, sent):
    def with_bit(number):
        return lambda value: lax.ppermute(
            value, "rep", [(i, i ^ 1 << number) for i in range(1 << PARTNERS)]
        )

    return lax.switch(bit % PARTNERS, [with_bit(n) for n in range(PARTNERS)], sent)


def body(
    cell_features, upstream, qkv_weight, out_weight, momentum, key_tiles, live_blocks, step_index
):
    step = step_index.reshape(1)
    layer_out, sent, theirs, velocity = run_layer(
        key_tiles[0], live_blocks[0], step,
        cell_features[0].reshape(TILES, TILE, D), upstream[0],
        qkv_weight[0], out_weight[0], momentum[0],
    )
    other = swap(step_index, sent)
    new_weight, new_momentum = average(step, velocity, other, out_weight[0], theirs)
    return layer_out[None], new_weight[None], new_momentum[None]


def solution(mesh):
    rows = P("rep", "shard", None)
    placed = (rows, rows, rows, rows, rows, P("rep", None, None), P("rep", None), P())
    return jax.shard_map(
        body, mesh=mesh, in_specs=placed, out_specs=(rows, rows, rows), check_vma=False
    )
```

```python
import functools

import jax
import jax.numpy as jnp
from jax import lax
from jax.experimental import pallas as pl
from jax.experimental.pallas import tpu as pltpu
from jax.sharding import PartitionSpec as P

HEADS = 16
HEAD_DIM = 64
TILE = 128
KB = 6
TILES = 4
NX = 4
NZ = 4
SHARDS = NX * NZ
PARTNERS = 4
GROUPS = NZ
D = 1024
GW = D // GROUPS
BLOCK = D // SHARDS
ROWS = TILES * TILE
MESH = pl.DeviceIdType.MESH

momentum_beta = 0.9


def at(z, x):
    return {"shard": z * NX + x}


def remote(src, dst, send, recv, device):
    return pltpu.make_async_remote_copy(
        src_ref=src, dst_ref=dst, send_sem=send, recv_sem=recv, device_id=device, device_id_type=MESH
    )


def layer_kernel(
    lists_ref, live_ref, step_ref, x_ref, up_ref, w_ref, ow_ref, mom_ref,
    layer_ref, sent_ref, theirs_ref, vel_ref,
    below0, below1, below2, above0, above1, above2,
    wparts, wbuf, owbuf, qbuf, kvbuf, mixed_out, att, grad, first, partial, second, total, theirs,
    ps, pr, cs, cr, ws, wr, zs, zr, ds, dr, es, er, as_, ar, gs, gr, hs, hr,
):
    me = lax.axis_index("shard")
    z, x = lax.div(me, NX), lax.rem(me, NX)
    right, left, far = (lax.rem(x + k, NX) for k in (1, NX - 1, NX // 2))
    ways = ((0, right, left), (1, left, right))

    def behind(away):
        return lax.rem(z - away + NZ, NZ)

    def ahead(away):
        return lax.rem(z + away, NZ)

    barrier = pltpu.get_barrier_semaphore()
    peers = [at(z, lax.rem(x + k, NX)) for k in range(1, NX)]
    peers += [at(lax.rem(z + k, NZ), x) for k in range(1, NZ)]
    rep = lax.axis_index("rep")
    partners = [
        rep + (1 << bit) * (1 - 2 * lax.rem(lax.div(rep, 1 << bit), 2)) for bit in range(PARTNERS)
    ]
    peers += [{"rep": other} for other in partners]
    for peer in peers:
        pl.semaphore_signal(barrier, 1, device_id=peer, device_id_type=MESH)
    for g in range(GROUPS):
        for part in range(3):
            wparts[g, :, pl.ds(part * GW, GW)] = w_ref[:, pl.ds(part * D + g * GW, GW)]
    wbuf[z, x] = wparts[z]
    owbuf[z, x] = ow_ref[...]
    pl.semaphore_wait(barrier, len(peers))

    def along_z(step, up, sending):
        came = z if sending else (z - 1 if up else z + 1)
        block = came - step if up else came + step
        valid = (block >= 0) & (block < NZ)
        if sending:
            valid &= (z < NZ - 1) if up else (z > 0)
        return valid, lax.rem(block + 2 * NZ, NZ), at(lax.rem(z + (1 if up else NZ - 1), NZ), x)

    W, OUT, PAIRS = 0, 1, (2, 3)

    def view(item, block, column, half=None):
        if item in PAIRS:
            base = (block * NX + column) * TILES + (item - PAIRS[0]) * 2
            return kvbuf.at[pl.ds(base, 2)] if half is None else kvbuf.at[pl.ds(base + half, 1)]
        ref = (wbuf if item == W else owbuf).at[block, column]
        return ref if half is None else ref.at[pl.ds(half * (BLOCK // 2), BLOCK // 2)]

    def x_copy(item, block, way, sending):
        _, to, back = ways[way]
        j = item * 8 + block * 2 + way
        ref = view(item, block, x if sending else back)
        return remote(ref, ref, ds.at[j], dr.at[j], at(z, to))

    def far_copy(item, block, way, sending):
        _, to, back = ways[way]
        j = item * 8 + block * 2 + way
        ref = view(item, block, back if sending else far, way)
        return remote(ref, ref, es.at[j], er.at[j], at(z, to))

    def share_x(item, block):
        for way in range(2):
            x_copy(item, block, way, True).start()

    def relay_x(item, block):
        for way in range(2):
            x_copy(item, block, way, False).wait_recv()
            far_copy(item, block, way, True).start()

    def finish_x(item):
        for block in range(NZ):
            for way in range(2):
                far_copy(item, block, way, False).wait_recv()

    def at_offset(offset, act):
        block = z + offset

        @pl.when((block >= 0) & (block < NZ))
        def _():
            act(lax.rem(block + NZ, NZ))

    def weight_copy(away, sending):
        to = ahead(away)
        return remote(
            wparts.at[to], wbuf.at[z if sending else behind(away), x],
            ws.at[away - 1], wr.at[away - 1], at(to, x),
        )

    blocks = {0: x_ref, -1: below0, -2: below1, -3: below2, 1: above0, 2: above1, 3: above2}

    def column_copy(t, step, up, sending):
        valid, _, to = along_z(step, up, sending)
        sign = -1 if up else 1
        j = (step * 2 + (0 if up else 1)) * TILES + t
        return valid, remote(
            blocks[sign * step].at[t], blocks[sign * (step + 1)].at[t], cs.at[j], cr.at[j], to
        )

    def start_column(t):
        for up in (True, False):
            valid, c = column_copy(t, 0, up, True)
            pl.when(valid)(c.start)

    def relay_column(t, step):
        for up in (True, False):
            valid, c = column_copy(t, step, up, False)

            @pl.when(valid)
            def _():
                c.wait_recv()
                if step + 1 < NZ - 1:
                    more, onward = column_copy(t, step + 1, up, True)
                    pl.when(more)(onward.start)

    def partner_copy(bit):
        return remote(ow_ref, theirs.at[bit], ps.at[bit], pr.at[bit], {"rep": partners[bit]})

    def out_copy(step, up, sending):
        valid, block, to = along_z(step, up, sending)
        j = step * 2 + (0 if up else 1)
        ref = owbuf.at[block, x]
        return valid, block, remote(ref, ref, zs.at[j], zr.at[j], to)

    def start_out():
        for up in (True, False):
            valid, _, c = out_copy(0, up, True)
            pl.when(valid)(c.start)

    def relay_out(step):
        for up in (True, False):
            valid, block, c = out_copy(step, up, False)

            @pl.when(valid)
            def _():
                c.wait_recv()
                if step + 1 < NZ - 1:
                    more, _, onward = out_copy(step + 1, up, True)
                    pl.when(more)(onward.start)
                share_x(OUT, block)

    def project(pair, block, rows):
        whole = jnp.dot(
            rows[pl.ds(pair * 2, 2)].reshape(2 * TILE, D), wbuf[...].reshape(D, 3 * GW),
            preferred_element_type=jnp.float32,
        ).astype(jnp.bfloat16).reshape(2, TILE, 3 * GW)
        base = pl.ds((block * NX + x) * TILES + pair * 2, 2)
        kvbuf[base, 0] = whole[:, :, GW : 2 * GW]
        kvbuf[base, 1] = whole[:, :, 2 * GW :]
        share_x(PAIRS[pair], block)
        qbuf[block, pl.ds(pair * 2, 2)] = whole[:, :, 0:GW] * jnp.bfloat16(HEAD_DIM ** -0.5)

    def both(distance, act):
        for offset in (-distance, distance):
            at_offset(offset, functools.partial(act, offset))

    def project_at(distance, pair):
        both(distance, lambda offset, block: project(pair, block, blocks[offset]))

    def relay_keys(distance, pair):
        both(distance, lambda offset, block: relay_x(PAIRS[pair], block))

    def relay_out_x(distance):
        both(distance, lambda offset, block: relay_x(OUT, block))

    for away in (1, 3, 2):
        weight_copy(away, True).start()
    share_x(W, z)
    share_x(OUT, z)
    for away in (1, 3):
        weight_copy(away, False).wait_recv()
        share_x(W, behind(away))
    start_column(0)
    weight_copy(2, False).wait_recv()
    share_x(W, behind(2))
    start_column(1)
    for away in (0, 1, 3, 2):
        relay_x(W, behind(away))
    start_column(2)
    finish_x(W)
    start_column(3)

    project(0, z, x_ref)
    relay_column(0, 0)
    project(1, z, x_ref)
    relay_x(PAIRS[0], z)
    relay_column(1, 0)
    project_at(1, 0)
    relay_x(PAIRS[1], z)
    relay_column(2, 0)
    relay_column(3, 0)
    project_at(1, 1)
    relay_column(0, 1)
    relay_keys(1, 0)
    relay_column(1, 1)
    project_at(2, 0)
    relay_keys(1, 1)
    relay_column(2, 1)
    relay_column(3, 1)
    project_at(2, 1)
    relay_keys(2, 0)
    relay_column(0, 2)
    relay_column(1, 2)
    start_out()
    for bit in range(PARTNERS):
        partner_copy(bit).start()
    project_at(3, 0)
    relay_keys(2, 1)
    relay_column(2, 2)
    relay_column(3, 2)
    project_at(3, 1)
    relay_out(0)
    relay_x(OUT, z)
    relay_keys(3, 0)
    relay_keys(3, 1)
    relay_out(1)
    for pair in PAIRS:
        finish_x(pair)

    lane_head = lax.broadcasted_iota(jnp.int32, (TILE, GW), 1) // HEAD_DIM
    slot_of = lax.broadcasted_iota(jnp.int32, (1, KB * TILE), 1) // TILE
    nt = (((1,), (1,)), ((), ()))
    tn = (((0,), (0,)), ((), ()))

    def mixed_copy(away, sending):
        return remote(
            mixed_out.at[away - 1], att.at[z if sending else behind(away)],
            as_.at[away - 1], ar.at[away - 1], at(ahead(away), x),
        )

    def attend(away):
        block = ahead(away)

        def one(i, c):
            tile = (block * NX + x) * TILES + i
            live = live_ref[tile]
            keys, values = [], []
            for j in range(KB):
                listed = lists_ref[tile, j]
                keys.append(kvbuf[listed, 0])
                values.append(kvbuf[listed, 1])
            q = qbuf[block, i]
            masked = jnp.concatenate(
                [jnp.where(lane_head == h, q, jnp.bfloat16(0)) for h in range(GW // HEAD_DIM)], axis=0
            )
            scores = lax.dot_general(
                masked, jnp.concatenate(keys, axis=0), nt, preferred_element_type=jnp.float32
            )
            scores = jnp.where(slot_of < live, scores, jnp.float32(-1e30))
            exponent = jnp.exp(scores - jnp.max(scores, axis=1, keepdims=True))
            scale = 1.0 / jnp.sum(exponent, axis=1, keepdims=True)
            mixed = jnp.dot(
                exponent.astype(jnp.bfloat16), jnp.concatenate(values, axis=0),
                preferred_element_type=jnp.float32,
            ) * scale
            joined = jnp.zeros((TILE, GW), jnp.float32)
            for h in range(GW // HEAD_DIM):
                joined = jnp.where(lane_head == h, mixed[h * TILE : (h + 1) * TILE], joined)
            joined = joined.astype(jnp.bfloat16)
            if away:
                mixed_out[away - 1, i] = joined
            else:
                att[z, i] = joined
            return c

        lax.fori_loop(0, TILES, one, 0, unroll=TILES)
        if away:
            mixed_copy(away, True).start()

    def first_copy(away, step):
        to = lax.rem(x + step, NX)
        i = away * (NX - 1) + step - 1
        return remote(
            grad.at[away, to], first.at[away, step - 1], gs.at[i], gr.at[i], at(z, to)
        )

    def second_copy(away):
        return remote(
            partial.at[away - 1], second.at[away - 1],
            hs.at[away - 1], hr.at[away - 1], at(behind(away), x),
        )

    def gradient(away):
        if away:
            mixed_copy(away, False).wait_recv()
        grad[away] = (
            lax.dot_general(
                att[behind(away)].reshape(ROWS, GW), up_ref[...], tn,
                preferred_element_type=jnp.float32,
            )
            .astype(jnp.bfloat16)
            .reshape(NX, BLOCK, D)
        )
        for step in range(1, NX):
            first_copy(away, step).start()

    def finish_first(away):
        summed = grad[away, x].astype(jnp.float32)
        for step in range(1, NX):
            first_copy(away, step).wait_recv()
            summed += first[away, step - 1].astype(jnp.float32)
        if away:
            partial[away - 1] = summed.astype(jnp.bfloat16)
            second_copy(away).start()
        else:
            total[...] = summed

    attend(2)
    relay_out(2)
    attend(1)
    relay_out_x(1)
    attend(3)
    attend(0)
    gradient(0)
    relay_out_x(2)
    relay_out_x(3)
    gradient(2)
    finish_first(0)
    gradient(1)
    finish_first(2)
    gradient(3)
    finish_first(1)

    def project_out(i, c):
        product = x_ref[i].astype(jnp.float32)
        for g in range(GROUPS):
            product += jnp.dot(
                att[g, i], owbuf[g].reshape(GW, D), preferred_element_type=jnp.float32
            )
        layer_ref[pl.ds(pl.multiple_of(i * TILE, TILE), TILE), :] = product.astype(jnp.bfloat16)
        return c

    finish_x(OUT)
    lax.fori_loop(0, TILES // 2, project_out, 0)
    finish_first(3)
    lax.fori_loop(TILES // 2, TILES, project_out, 0)

    summed = total[...]
    for away in range(1, NZ):
        second_copy(away).wait_recv()
        summed += second[away - 1].astype(jnp.float32)
    velocity = momentum_beta * mom_ref[...] + summed
    vel_ref[...] = velocity
    sent_ref[...] = velocity.astype(jnp.bfloat16)
    for bit in range(PARTNERS):
        partner_copy(bit).wait_recv()
    theirs_ref[...] = theirs[lax.rem(step_ref[0], PARTNERS)]

    for item in range(4):
        for block in range(NZ):
            for way in range(2):
                x_copy(item, block, way, True).wait_send()
                far_copy(item, block, way, True).wait_send()
    for step in range(NZ - 1):
        for up in (True, False):
            valid, _, c = out_copy(step, up, True)
            pl.when(valid)(c.wait_send)
            for t in range(TILES):
                valid, c = column_copy(t, step, up, True)
                pl.when(valid)(c.wait_send)
    for away in range(1, NZ):
        weight_copy(away, True).wait_send()
        mixed_copy(away, True).wait_send()
        second_copy(away).wait_send()
    for away in range(NZ):
        for step in range(1, NX):
            first_copy(away, step).wait_send()
    for bit in range(PARTNERS):
        partner_copy(bit).wait_send()


def run_layer(lists, live, step, features, upstream, qkv, out, momentum):
    vmem = pl.BlockSpec(memory_space=pltpu.VMEM)
    smem = pl.BlockSpec(memory_space=pltpu.SMEM)
    bf16, f32 = jnp.bfloat16, jnp.float32

    def sems(count):
        return [pltpu.SemaphoreType.DMA((count,))] * 2

    return pl.pallas_call(
        layer_kernel,
        name="layer",
        out_shape=(
            jax.ShapeDtypeStruct((ROWS, D), bf16),
            jax.ShapeDtypeStruct((BLOCK, D), bf16),
            jax.ShapeDtypeStruct((BLOCK, D), bf16),
            jax.ShapeDtypeStruct((BLOCK, D), f32),
        ),
        in_specs=[smem] * 3 + [vmem] * 5,
        out_specs=(vmem,) * 4,
        scratch_shapes=[
            *[pltpu.VMEM((TILES, TILE, D), bf16)] * 6,
            pltpu.VMEM((GROUPS, BLOCK, 3 * GW), bf16),
            pltpu.VMEM((NZ, NX, BLOCK, 3 * GW), bf16),
            pltpu.VMEM((NZ, NX, BLOCK, D), bf16),
            pltpu.VMEM((NZ, TILES, TILE, GW), bf16),
            pltpu.VMEM((SHARDS * TILES, 2, TILE, GW), bf16),
            pltpu.VMEM((NZ - 1, TILES, TILE, GW), bf16),
            pltpu.VMEM((GROUPS, TILES, TILE, GW), bf16),
            pltpu.VMEM((GROUPS, NX, BLOCK, D), bf16),
            pltpu.VMEM((GROUPS, NX - 1, BLOCK, D), bf16),
            pltpu.VMEM((NZ - 1, BLOCK, D), bf16),
            pltpu.VMEM((NZ - 1, BLOCK, D), bf16),
            pltpu.VMEM((BLOCK, D), f32),
            pltpu.VMEM((PARTNERS, BLOCK, D), bf16),
            *sems(PARTNERS), *sems(6 * TILES), *sems(NZ - 1), *sems(6), *sems(8 * 4), *sems(8 * 4),
            *sems(NZ - 1), *sems(GROUPS * (NX - 1)), *sems(NZ - 1),
        ],
        compiler_params=pltpu.CompilerParams(
            collective_id=0, has_side_effects=True, vmem_limit_bytes=58 * 2**20
        ),
    )(lists, live, step, features, upstream, qkv, out, momentum)


def average(step_index, velocity, other, out, other_out):
    rate = jnp.float32(50.0) / (jnp.float32(500.0) + step_index.astype(jnp.float32))
    other = other.astype(jnp.float32)

    def stepped(weight, moved):
        moved = weight.astype(jnp.float32) - rate * moved
        return moved.astype(jnp.bfloat16).astype(jnp.float32)

    both = stepped(out, velocity) + stepped(other_out, other)
    return (0.5 * both).astype(jnp.bfloat16), 0.5 * (velocity + other)


def swap(bit, sent):
    def with_bit(number):
        return lambda value: lax.ppermute(
            value, "rep", [(i, i ^ 1 << number) for i in range(1 << PARTNERS)]
        )

    return lax.switch(bit % PARTNERS, [with_bit(n) for n in range(PARTNERS)], sent)


def body(
    cell_features, upstream, qkv_weight, out_weight, momentum, key_tiles, live_blocks, step_index
):
    step = step_index.reshape(1)
    layer_out, sent, theirs, velocity = run_layer(
        key_tiles[0], live_blocks[0], step,
        cell_features[0].reshape(TILES, TILE, D), upstream[0],
        qkv_weight[0], out_weight[0], momentum[0],
    )
    other = swap(step_index, sent)
    new_weight, new_momentum = average(step_index, velocity, other, out_weight[0], theirs)
    return layer_out[None], new_weight[None], new_momentum[None]


def solution(mesh):
    rows = P("rep", "shard", None)
    placed = (rows, rows, rows, rows, rows, P("rep", None, None), P("rep", None), P())
    return jax.shard_map(
        body, mesh=mesh, in_specs=placed, out_specs=(rows, rows, rows), check_vma=False
    )
```
